32 devices in a mesh: gx: 8 (over y, x, core), gy: 4 (over z).
Axes of the slice: x: 2, y: 2, z: 4, core: 2. Of those that a mesh axis runs over, the one named last changes fastest.
Arguments:
- test_vectors: float32 [5, 64, 4096], P(None, None, ('gx', 'gy')), may hold values from -1100 to 1100
- face_jacobians: float32 [4, 5, 5], replicated, may hold values from -2.4 to 2.4
- wave_speed: float32 [4096], P(('gx', 'gy')), may hold values from 0.5 to 2
- viscosity: float32 [4096], P(('gx', 'gy')), may hold values from 0.05 to 0.5
- inverse_volume: float32 [4096], P(('gx', 'gy')), may hold values from 0.5 to 2
- connectivity: int32 [4, 4096], P(None, ('gx', 'gy')), may hold values from 0 to 192, as said below
- send_rows: int32 [4, 512], P(None, ('gx', 'gy')), may hold values from 0 to 127, as said below
- cell_count: int32 [32], P(('gx', 'gy')), may hold values from 64 to 128, as said below
Outputs:
- basis_vectors: float32 [5, 64, 4096], P(None, None, ('gx', 'gy'))
- factor: float32 [64, 64], replicated
The draws below stay inside these ranges and needn't reach their ends.
Inputs may be any that keep to these rules, and one draw needn't show every extreme that they name: `cell_count`: one partition holds exactly 128 live cells and one exactly 64. `send_rows`: entries of partition p's lists name its owned cells below cell_count[p]; list 0 goes to the partition one row lower, 1 one row higher, 2 one column lower, 3 one column higher; every slot is sent, used or not. `connectivity`: an entry below 128 is a live owned cell; 128 + b * 16 + s is slot s of ghost block b, used only where that neighbouring partition exists; 192 is the far field (zero perturbation). How many slots of a block are used varies by partition and direction.
All inputs are finite; a program needn't handle non-finite values.
Results may differ from the reference program's by a relative error of at most 0.0001.
Values sent between devices are 32-bit elements; how exact they have to be, the bound alone decides.
No kernel may reach another device: no remote copies, remote signals or barrier semaphores. Data moves between devices by JAX's collectives and lax.ppermute only.
A program may use at most 64 MiB of HBM per device.

```python
import math
import jax
import jax.numpy as jnp
from jax import lax

FIELDS = 5
VECS = 64
FACES = 4
C_MAX = 128
G_SLOTS = 16
PART_ROWS = 8
PART_COLS = 4
PARTS_SIZE = 32
NCELLS = 4096


def live_counts(key):
    subkeys = jax.random.split(jax.random.fold_in(key, 11), 2)
    counts = jax.random.randint(subkeys[0], (PARTS_SIZE,), C_MAX // 2, C_MAX + 1)
    shuffled = jax.random.permutation(subkeys[1], PARTS_SIZE)
    counts = counts.at[shuffled[0]].set(C_MAX).at[shuffled[1]].set(C_MAX // 2)
    return counts.astype(jnp.int32)


def draw_cell_count(key, part):
    return live_counts(key)


def draw_send_rows(key, part):
    counts = live_counts(key)
    subkeys = jax.random.split(jax.random.fold_in(key, 31), 2)
    listed = jax.random.randint(subkeys[0], (FACES, PARTS_SIZE, G_SLOTS), 0, counts[None, :, None])
    forced_slot = jax.random.randint(subkeys[1], (FACES, PARTS_SIZE), 0, G_SLOTS)
    slot_grid = jnp.arange(G_SLOTS, dtype=jnp.int32)[None, None, :]
    listed = jnp.where(slot_grid == forced_slot[:, :, None], counts[None, :, None] - 1, listed)
    return listed.reshape(FACES, PARTS_SIZE * G_SLOTS).astype(jnp.int32)


def draw_connectivity(key, part):
    counts = live_counts(key)
    subkeys = jax.random.split(jax.random.fold_in(key, 47), 6)
    used_slots = jax.random.randint(subkeys[0], (PARTS_SIZE, FACES), max(1, G_SLOTS // 4), G_SLOTS + 1)
    full_part = jax.random.randint(subkeys[1], (), 0, PARTS_SIZE)
    full_face = jax.random.randint(subkeys[2], (), 0, FACES)
    used_slots = used_slots.at[full_part, full_face].set(G_SLOTS)
    face_kind = jax.random.randint(subkeys[3], (FACES, PARTS_SIZE, C_MAX), 0, 10)
    local_index = jax.random.randint(subkeys[4], (FACES, PARTS_SIZE, C_MAX), 0, counts[None, :, None])
    direction = jnp.clip(face_kind - 6, 0, 3)
    part_index = jnp.arange(PARTS_SIZE, dtype=jnp.int32)
    slot_limit = used_slots[part_index[None, :, None], direction]
    slot_index = jax.random.randint(subkeys[5], (FACES, PARTS_SIZE, C_MAX), 0, slot_limit)
    part_row = part_index // PART_COLS
    part_col = part_index % PART_COLS
    exists = jnp.stack([part_row > 0, part_row < PART_ROWS - 1, part_col > 0, part_col < PART_COLS - 1], axis=1)
    exists_here = exists[part_index[None, :, None], direction]
    ghost_index = C_MAX + direction * G_SLOTS + slot_index
    boundary = C_MAX + FACES * G_SLOTS
    neighbors = jnp.where(face_kind < 6, local_index, jnp.where(exists_here, ghost_index, boundary))
    return neighbors.reshape(FACES, PARTS_SIZE * C_MAX).astype(jnp.int32)


def draw_test_vectors(key, part):
    subkeys = jax.random.split(key, 3)
    cell_scale = jnp.exp(jax.random.uniform(subkeys[0], (NCELLS,), jnp.float32, 0.0, math.log(10.0)))
    column_scale = jnp.exp(jax.random.uniform(subkeys[1], (VECS,), jnp.float32, 0.0, math.log(10.0)))
    device_ramp = 3.0 ** (0.5 * (jnp.arange(NCELLS) // C_MAX).astype(jnp.float32) / (PARTS_SIZE - 1))
    base_draw = jax.random.normal(subkeys[2], (FIELDS, VECS, NCELLS), jnp.float32)
    base_draw = jnp.clip(base_draw, -6.0, 6.0)
    scaled = base_draw * (cell_scale * device_ramp)[None, None, :] * column_scale[None, :, None]
    return scaled.astype(jnp.float32)


def shard_levels(key, extent, cuts, low, high):
    def one(position, parts):
        heights = jax.random.uniform(jax.random.fold_in(jax.random.fold_in(key, 6), position), (parts,), jnp.float32, low / len(cuts), high / len(cuts))
        return jnp.repeat(jnp.exp(heights), extent[position] // parts).reshape((-1,) + (1,) * (len(extent) - position - 1))

    factor_of = one(*cuts[0])
    for cut in cuts[1:]:
        factor_of = factor_of * one(*cut)
    return factor_of


def normal_values(own_key, extent, width, bound, kind=jnp.bfloat16):
    return jnp.clip(width * jax.random.normal(own_key, extent, jnp.float32), -bound, bound).astype(kind)


def setup_inputs(seed: int = 0) -> dict:
    seeds = jax.random.split(jax.random.key(seed), 9)
    return {
        "test_vectors": draw_test_vectors(jax.random.fold_in(seeds[8], 71), 0),
        "face_jacobians": normal_values(seeds[1], (FACES, FIELDS, FIELDS), 0.4, 2.4, jnp.float32),
        "wave_speed": jnp.clip(jnp.exp(math.log(2.0) - 1.3862944 * jax.random.uniform(seeds[2], (NCELLS,), jnp.float32) ** shard_levels(seeds[2], (NCELLS,), ((0, 32),), -0.2, 0.2)), 0.5, 2.0),
        "viscosity": jnp.clip(jnp.exp(math.log(0.5) - 2.3025851 * jax.random.uniform(seeds[3], (NCELLS,), jnp.float32) ** shard_levels(seeds[3], (NCELLS,), ((0, 32),), -0.2, 0.2)), 0.05, 0.5),
        "inverse_volume": jnp.clip(jnp.exp(math.log(2.0) - 1.3862944 * jax.random.uniform(seeds[4], (NCELLS,), jnp.float32) ** shard_levels(seeds[4], (NCELLS,), ((0, 32),), -0.2, 0.2)), 0.5, 2.0),
        "connectivity": draw_connectivity(jax.random.fold_in(seeds[8], 71), 0),
        "send_rows": draw_send_rows(jax.random.fold_in(seeds[8], 71), 0),
        "cell_count": draw_cell_count(jax.random.fold_in(seeds[8], 71), 0),
    }


time_step = 0.4

def shifted(blocks, along, forward):
    length = blocks.shape[along]
    zero_block = jnp.zeros_like(lax.slice_in_dim(blocks, 0, 1, axis=along))
    if forward:
        return jnp.concatenate([zero_block, lax.slice_in_dim(blocks, 0, length - 1, axis=along)], axis=along)
    return jnp.concatenate([lax.slice_in_dim(blocks, 1, length, axis=along), zero_block], axis=along)

def take_rows(current, rows):
    return jnp.take(current, rows, axis=2)

def cell_operator(extended, connect, face_jacobians, wave_speed, viscosity, inverse_volume):
    owned_cells = connect.shape[1]
    own_state = extended[:, :, :owned_cells]
    advection = jnp.zeros(own_state.shape, jnp.float32)
    diffusion = jnp.zeros(own_state.shape, jnp.float32)
    for face_index in range(4):
        neighbor = jnp.take(extended, connect[face_index], axis=2)
        advection = advection + jnp.einsum('ij,jvc->ivc', face_jacobians[face_index], neighbor, precision=lax.Precision.HIGHEST)
        diffusion = diffusion + neighbor
    return inverse_volume * (-0.5 * wave_speed * advection + viscosity * (diffusion - 4.0 * own_state))

def apply_operator(current, face_jacobians, wave_speed, viscosity, inverse_volume, connect, sends):
    outgoing = jax.vmap(jax.vmap(take_rows))(current, sends)
    from_lower_row = shifted(outgoing[:, :, :, :, 1, :], 0, True)
    from_upper_row = shifted(outgoing[:, :, :, :, 0, :], 0, False)
    from_lower_col = shifted(outgoing[:, :, :, :, 3, :], 1, True)
    from_upper_col = shifted(outgoing[:, :, :, :, 2, :], 1, False)
    zero_block = jnp.zeros(current.shape[:4] + (1,), jnp.float32)
    extended = jnp.concatenate([current, from_lower_row, from_upper_row, from_lower_col, from_upper_col, zero_block], axis=4)

    def row_operator(inputs):
        ext_row, conn_row, speed_row, visc_row, volume_row = inputs
        return jax.vmap(cell_operator, in_axes=(0, 0, None, 0, 0, 0))(ext_row, conn_row, face_jacobians, speed_row, visc_row, volume_row)
    return lax.map(row_operator, (extended, connect, wave_speed, viscosity, inverse_volume))

def reference(test_vectors, face_jacobians, wave_speed, viscosity, inverse_volume, connectivity, send_rows, cell_count):
    current = test_vectors.reshape(FIELDS, VECS, PART_ROWS, PART_COLS, C_MAX).transpose(2, 3, 0, 1, 4)
    connect = connectivity.reshape(FACES, PART_ROWS, PART_COLS, C_MAX).transpose(1, 2, 0, 3)
    sends = send_rows.reshape(FACES, PART_ROWS, PART_COLS, G_SLOTS).transpose(1, 2, 0, 3)
    speed_cells = wave_speed.reshape(PART_ROWS, PART_COLS, C_MAX)[:, :, None, None, :]
    visc_cells = viscosity.reshape(PART_ROWS, PART_COLS, C_MAX)[:, :, None, None, :]
    volume_cells = inverse_volume.reshape(PART_ROWS, PART_COLS, C_MAX)[:, :, None, None, :]

    def operate(state_now):
        return apply_operator(state_now, face_jacobians, speed_cells, visc_cells, volume_cells, connect, sends)
    section_one = operate(current)
    section_two = operate(current + 0.5 * time_step * section_one)
    section_three = operate(current + 0.5 * time_step * section_two)
    section_four = operate(current + time_step * section_three)
    advanced = current + time_step / 6.0 * (section_one + 2.0 * section_two + 2.0 * section_three + section_four)
    live_mask = (jnp.arange(C_MAX, dtype=jnp.int32)[None, None, :] < cell_count.reshape(PART_ROWS, PART_COLS)[:, :, None]).astype(jnp.float32)
    advanced = advanced * live_mask[:, :, None, None, :]
    gram_whole = jnp.einsum('abfic,abfjc->ij', advanced, advanced, precision=lax.Precision.HIGHEST)
    gram_whole = gram_whole / float(FIELDS * NCELLS)
    lower_factor = jnp.linalg.cholesky(gram_whole)
    inverse_lower = jax.scipy.linalg.solve_triangular(lower_factor, jnp.eye(VECS, dtype=jnp.float32), lower=True)
    basis_out = jnp.einsum('ij,abfjc->abfic', inverse_lower, advanced, precision=lax.Precision.HIGHEST)
    basis_out = basis_out.transpose(2, 3, 0, 1, 4).reshape(FIELDS, VECS, NCELLS)
    return (basis_out, lower_factor.T)
```

```python
import functools

import jax
import jax.numpy as jnp
from jax import lax
from jax.experimental import pallas as pl
from jax.experimental.pallas import tpu as pltpu
from jax.sharding import PartitionSpec as P

time_step = 0.4
lanes = 128
sublanes = 8
HIGHEST = lax.Precision.HIGHEST


def partner(index, count, odd):
    other = index + 1 if index % 2 == odd else index - 1
    return other if 0 <= other < count else None


def matchings(rows, cols):
    row_even, row_odd, col_even, col_odd = [], [], [], []
    for i in range(rows):
        for j in range(cols):
            here = i * cols + j
            row_even.append((here, (i ^ 1) * cols + j))
            col_even.append((here, i * cols + (j ^ 1)))
            up = partner(i, rows, 1)
            row_odd.append((here, (rows - 1 - i if up is None else up) * cols + j))
            across = partner(j, cols, 1)
            col_odd.append((here, (i ^ 1) * cols + j if across is None else i * cols + across))
    return row_even, row_odd, col_even, col_odd


def lane_take(values, index):
    return jnp.take_along_axis(values, index, axis=1, mode="promise_in_bounds")


def swapped(lists, row_swap, col_swap):
    first, second, third, fourth = lists
    return [
        jnp.where(row_swap, second, first),
        jnp.where(row_swap, first, second),
        jnp.where(col_swap, fourth, third),
        jnp.where(col_swap, third, fourth),
    ]


def lane_ids():
    return lax.broadcasted_iota(jnp.int32, (sublanes, lanes), 1)


def send_index(send_ref, flags_ref, slots):
    lane = lane_ids()
    index = jnp.zeros((sublanes, lanes), jnp.int32)
    for b in range(4):
        swap = flags_ref[b // 2]
        source = jnp.bitwise_xor(b, swap)
        for s in range(slots):
            index = jnp.where(lane == b * slots + s, send_ref[source, s], index)
    return index


def pack(states, base_index, out_refs, groups, slots):
    group = lane_ids() // slots
    fields = len(states[0])
    packed = [[None] * fields for _ in range(4)]
    for m in range(groups):
        index = pltpu.roll(base_index, m * slots, 1) if m else base_index
        for f in range(fields):
            taken = lane_take(states[m][f], index)
            for b in range(4):
                before = packed[b][f]
                packed[b][f] = (
                    taken
                    if before is None
                    else jnp.where(group == (m + b) % groups, taken, before)
                )
    for b in range(4):
        for f in range(fields):
            out_refs[b][f] = packed[b][f]


def pack_kernel(flags_ref, send_ref, q_ref, *out_refs):
    fields, vectors, _ = q_ref.shape
    slots = send_ref.shape[1]
    groups = lanes // slots
    base_index = send_index(send_ref, flags_ref, slots)
    states = [
        [q_ref[f, pl.ds(m * sublanes, sublanes), :] for f in range(fields)] for m in range(groups)
    ]
    pack(states, base_index, out_refs, groups, slots)


def stage_kernel(
    stage,
    flags_ref,
    send_ref,
    jac_ref,
    count_ref,
    conn_ref,
    speed_ref,
    visc_ref,
    volume_ref,
    q_ref,
    *refs,
):
    refs = list(refs)
    state_ref = q_ref if stage == 0 else refs.pop(0)
    acc_ref = q_ref if stage == 0 else refs.pop(0)
    recv_refs = [refs.pop(0) for _ in range(4)]
    fields, vectors, cells = q_ref.shape
    slots = send_ref.shape[1]
    groups = lanes // slots
    lane = lane_ids()
    group = lane // slots
    shape = (sublanes, lanes)

    weight = jnp.broadcast_to(volume_ref[...], shape)
    advect = -0.5 * jnp.broadcast_to(speed_ref[...], shape) * weight
    diffuse = jnp.broadcast_to(visc_ref[...], shape) * weight
    row_swap = flags_ref[0] * slots
    col_swap = flags_ref[1] * slots
    own_index, ghost_index, is_ghost = [], [], []
    for face in range(4):
        entry = jnp.broadcast_to(conn_ref[pl.ds(face, 1), :], shape)
        ghost = entry - cells
        ghost = jnp.where(
            ghost < 2 * slots,
            jnp.bitwise_xor(ghost, row_swap),
            jnp.where(ghost < 4 * slots, jnp.bitwise_xor(ghost, col_swap), ghost),
        )
        own_index.append(jnp.bitwise_and(entry, lanes - 1))
        ghost_index.append(ghost)
        is_ghost.append(entry >= cells)

    last = stage == 3
    kept_coef = time_step / 6.0 if stage in (0, 3) else time_step / 3.0
    next_coef = (0.5 * time_step, 0.5 * time_step, time_step, None)[stage]
    if last:
        live = lane < count_ref[0]
        advanced_ref, gram_ref, wide_ref = refs
    else:
        next_ref, next_acc_ref, *out_refs = refs
    states = []
    zero = jnp.zeros(shape, jnp.float32)
    for m in range(groups):
        rows = pl.ds(m * sublanes, sublanes)
        own = [state_ref[f, rows, :] for f in range(fields)]
        ghosts = []
        for f in range(fields):
            block = zero
            for b in range(4):
                block = jnp.where(group == (m + b) % groups, recv_refs[b][f], block)
            ghosts.append(block)
        advection = [None] * fields
        diffusion = [-4.0 * own[f] for f in range(fields)]
        for face in range(4):
            index = jnp.bitwise_and(ghost_index[face] + m * slots, lanes - 1)
            near = []
            for f in range(fields):
                near.append(
                    jnp.where(
                        is_ghost[face],
                        lane_take(ghosts[f], index),
                        lane_take(own[f], own_index[face]),
                    )
                )
                diffusion[f] = diffusion[f] + near[f]
            for i in range(fields):
                for j in range(fields):
                    term = jac_ref[face, i * fields + j] * near[j]
                    advection[i] = term if advection[i] is None else advection[i] + term
        following = []
        for f in range(fields):
            slope = advect * advection[f] + diffuse * diffusion[f]
            kept = acc_ref[f, rows, :] + kept_coef * slope
            if last:
                advanced_ref[f, rows, :] = jnp.where(live, kept, 0.0)
            else:
                next_acc_ref[f, rows, :] = kept
                after = q_ref[f, rows, :] + next_coef * slope
                next_ref[f, rows, :] = after
                following.append(after)
        states.append(following)
    if not last:
        pack(states, send_index(send_ref, flags_ref, slots), out_refs, groups, slots)
        return
    half = vectors // 2
    wide_ref[...] = jnp.zeros(wide_ref.shape, jnp.float32)
    total = None
    for f in range(fields):
        wide_ref[pl.ds(0, vectors), :] = advanced_ref[f]
        wide_ref[pl.ds(vectors, vectors), :] = jnp.zeros((vectors, lanes), jnp.float32)
        low = wide_ref[...]
        high = jnp.concatenate([low[vectors:], low[:vectors]], axis=0)
        for left, right in ((low[:half], low), (low[half:vectors], high)):
            part = lax.dot_general(
                left,
                right,
                (((1,), (1,)), ((), ())),
                precision=HIGHEST,
                preferred_element_type=jnp.float32,
            )
            total = part if total is None else total + part
    gram_ref[...] = total


def factor_kernel(scale, gram_ref, advanced_ref, basis_ref, factor_ref):
    fields, vectors, cells = advanced_ref.shape
    half = vectors // 2
    folded = gram_ref[...] * scale
    turned = pltpu.roll(folded, vectors, 1)
    work = jnp.concatenate([folded, turned], axis=0)
    row = lax.broadcasted_iota(jnp.int32, (vectors, lanes), 0)
    lane = lax.broadcasted_iota(jnp.int32, (vectors, lanes), 1)
    work = jnp.where(lane < vectors, work, jnp.where(lane == row + vectors, 1.0, 0.0))
    blocks = [work[b * sublanes : (b + 1) * sublanes] for b in range(vectors // sublanes)]
    sub = lax.broadcasted_iota(jnp.int32, (sublanes, lanes), 0)
    scales = []
    for b in range(len(blocks)):
        start = b * sublanes
        count = len(blocks) - b
        columns = [
            [
                jnp.broadcast_to(blocks[c][:, start + k : start + k + 1], (sublanes, lanes))
                for c in range(b, len(blocks))
            ]
            for k in range(sublanes)
        ]
        for k in range(sublanes):
            pivot = jnp.broadcast_to(columns[k][0][k : k + 1], (sublanes, lanes))
            scales.append(pivot)
            inverse = 1.0 / pivot
            row_k = jnp.broadcast_to(blocks[b][k : k + 1], (sublanes, lanes)) * inverse
            later = [
                jnp.broadcast_to(columns[n][0][k : k + 1], (sublanes, lanes)) * inverse
                for n in range(k + 1, sublanes)
            ]
            for c in range(count):
                ratio = columns[k][c]
                if c == 0:
                    ratio = jnp.where(sub > k, ratio, 0.0)
                blocks[b + c] = blocks[b + c] - ratio * row_k
                for n in range(k + 1, sublanes):
                    columns[n][c] = columns[n][c] - ratio * later[n - k - 1]
    for b in range(len(blocks)):
        pivots = scales[b * sublanes]
        for k in range(1, sublanes):
            pivots = jnp.where(sub == k, scales[b * sublanes + k], pivots)
        blocks[b] = blocks[b] * lax.rsqrt(pivots)
    done = jnp.concatenate(blocks, axis=0)
    factor_ref[...] = jnp.where(lane >= row, done, 0.0)[:, :vectors]
    inverse_lower = pltpu.roll(done, vectors, 1)[:, :vectors]
    for f in range(fields):
        basis_ref[f] = jnp.dot(
            inverse_lower,
            advanced_ref[f],
            precision=HIGHEST,
            preferred_element_type=jnp.float32,
        )


def summed(value, axes):
    for axis, size, pair_first in axes:
        bits = size.bit_length() - 1
        at = 0
        while at < bits:
            width = 1 if (pair_first and at == 0) else min(2, bits - at)
            parts = [value]
            for k in range(1, 1 << width):
                step = k << at
                parts.append(lax.ppermute(value, axis, [(i, i ^ step) for i in range(size)]))
            while len(parts) > 1:
                parts = [parts[i] + parts[i + 1] for i in range(0, len(parts), 2)]
            value = parts[0]
            at += width
    return value


def shards(
    mesh_shape,
    test_vectors,
    face_jacobians,
    wave_speed,
    viscosity,
    inverse_volume,
    connectivity,
    send_rows,
    cell_count,
):
    rows, cols = mesh_shape
    fields, vectors, cells = test_vectors.shape
    slots = send_rows.shape[1]
    assert cells == lanes and vectors * slots == sublanes * lanes and 2 * vectors == lanes
    vmem = pl.BlockSpec(memory_space=pltpu.VMEM)
    smem = pl.BlockSpec(memory_space=pltpu.SMEM)
    flags = jnp.stack(
        [1 - lax.axis_index("gx") % 2, 1 - lax.axis_index("gy") % 2]
    ).astype(jnp.int32)
    jacobians = face_jacobians.reshape(4, fields * fields)
    speed = wave_speed.reshape(1, cells)
    visc = viscosity.reshape(1, cells)
    volume = inverse_volume.reshape(1, cells)
    state = jax.ShapeDtypeStruct(test_vectors.shape, jnp.float32)
    block = jax.ShapeDtypeStruct((fields, sublanes, lanes), jnp.float32)
    params = pltpu.CompilerParams(vmem_limit_bytes=16 * 1024 * 1024)
    pairs = matchings(rows, cols)

    def exchange(sent):
        got = [None] * 4
        for which in (0, 3, 2, 1):
            got[which] = lax.ppermute(sent[which], ("gx", "gy"), pairs[which])
        return got

    sent = pl.pallas_call(
        pack_kernel,
        out_shape=[block] * 4,
        in_specs=[smem, smem, vmem],
        out_specs=[vmem] * 4,
        compiler_params=params,
        name="pack",
    )(flags, send_rows, test_vectors)
    held = []
    for stage in range(4):
        got = exchange(sent)
        last = stage == 3
        gram_shape = jax.ShapeDtypeStruct((vectors // 2, lanes), jnp.float32)
        result = pl.pallas_call(
            functools.partial(stage_kernel, stage),
            out_shape=[state, gram_shape] if last else [state, state] + [block] * 4,
            in_specs=[smem] * 4 + [vmem] * (5 + len(held) + 4),
            out_specs=[vmem] * (2 if last else 6),
            scratch_shapes=[pltpu.VMEM((2 * vectors, lanes), jnp.float32)] if last else [],
            compiler_params=params,
            name="stage",
        )(
            flags,
            send_rows,
            jacobians,
            cell_count,
            connectivity,
            speed,
            visc,
            volume,
            test_vectors,
            *held,
            *got,
        )
        held, sent = result[:2], result[2:]
    advanced, gram = held
    gram = summed(gram, (("gx", rows, True), ("gy", cols, False)))
    scale = 1.0 / float(fields * cells * rows * cols)
    return pl.pallas_call(
        functools.partial(factor_kernel, scale),
        out_shape=[state, jax.ShapeDtypeStruct((vectors, vectors), jnp.float32)],
        in_specs=[vmem] * 2,
        out_specs=[vmem] * 2,
        compiler_params=params,
        name="factor",
    )(gram, advanced)


def solution(mesh):
    placed = (
        P(None, None, ("gx", "gy")),
        P(),
        P(("gx", "gy")),
        P(("gx", "gy")),
        P(("gx", "gy")),
        P(None, ("gx", "gy")),
        P(None, ("gx", "gy")),
        P(("gx", "gy")),
    )
    return jax.shard_map(
        functools.partial(shards, (mesh.shape["gx"], mesh.shape["gy"])),
        mesh=mesh,
        in_specs=placed,
        out_specs=(P(None, None, ("gx", "gy")), P()),
        check_vma=False,
    )
```

```python
import functools

import jax
import jax.numpy as jnp
from jax import lax
from jax.experimental import pallas as pl
from jax.experimental.pallas import tpu as pltpu
from jax.sharding import PartitionSpec as P

time_step = 0.4
lanes = 128
sublanes = 8
HIGHEST = lax.Precision.HIGHEST


def partner(index, count, odd):
    other = index + 1 if index % 2 == odd else index - 1
    return other if 0 <= other < count else None


def matchings(rows, cols):
    row_even, row_odd, col_even, col_odd = [], [], [], []
    for i in range(rows):
        for j in range(cols):
            here = i * cols + j
            row_even.append((here, (i ^ 1) * cols + j))
            col_even.append((here, i * cols + (j ^ 1)))
            up = partner(i, rows, 1)
            row_odd.append((here, (rows - 1 - i if up is None else up) * cols + j))
            across = partner(j, cols, 1)
            col_odd.append((here, (i ^ 1) * cols + j if across is None else i * cols + across))
    return row_even, row_odd, col_even, col_odd


def lane_take(values, index):
    return jnp.take_along_axis(values, index, axis=1, mode="promise_in_bounds")


def lane_ids():
    return lax.broadcasted_iota(jnp.int32, (sublanes, lanes), 1)


def pack(states, send_table_ref, out_refs, groups, slots):
    group = lane_ids() // slots
    fields = len(states[0])
    packed = [[None] * fields for _ in range(4)]
    for m in range(groups):
        index = send_table_ref[pl.ds(m * sublanes, sublanes), :]
        for f in range(fields):
            taken = lane_take(states[m][f], index)
            for b in range(4):
                before = packed[b][f]
                packed[b][f] = (
                    taken
                    if before is None
                    else jnp.where(group == (m + b) % groups, taken, before)
                )
    for b in range(4):
        for f in range(fields):
            out_refs[b][f] = packed[b][f]


def prepare_kernel(send_ref, q_ref, send_table_ref, *out_refs):
    fields, vectors, cells = q_ref.shape
    slots = send_ref.shape[1]
    groups = lanes // slots
    shape = (sublanes, lanes)
    row_even = lax.axis_index("gx") % 2 == 0
    col_even = lax.axis_index("gy") % 2 == 0
    sends = jnp.concatenate(
        [send_ref[...], jnp.zeros((4, lanes - slots), jnp.int32)], axis=1
    )
    spread = [jnp.broadcast_to(sends[b : b + 1], shape) for b in range(4)]
    ordered = [
        jnp.where(row_even, spread[1], spread[0]),
        jnp.where(row_even, spread[0], spread[1]),
        jnp.where(col_even, spread[3], spread[2]),
        jnp.where(col_even, spread[2], spread[3]),
    ]
    base = ordered[0]
    for b in range(1, 4):
        base = jnp.where(lane_ids() // slots == b, pltpu.roll(ordered[b], b * slots, 1), base)
    for m in range(groups):
        send_table_ref[pl.ds(m * sublanes, sublanes), :] = (
            pltpu.roll(base, m * slots, 1) if m else base
        )
    states = [
        [q_ref[f, pl.ds(m * sublanes, sublanes), :] for f in range(fields)] for m in range(groups)
    ]
    pack(states, send_table_ref, out_refs, groups, slots)


def tables_kernel(
    slots,
    count_ref,
    jac_ref,
    conn_ref,
    speed_ref,
    visc_ref,
    volume_ref,
    weight_ref,
    entry_ref,
    ghost_ref,
    splat_ref,
):
    cells = conn_ref.shape[1]
    fields = jac_ref.shape[1]
    shape = (sublanes, lanes)
    groups = lanes // slots
    row_swap = jnp.where(lax.axis_index("gx") % 2 == 0, slots, 0)
    col_swap = jnp.where(lax.axis_index("gy") % 2 == 0, slots, 0)
    volume = jnp.broadcast_to(volume_ref[...], shape)
    weight_ref[0] = -0.5 * jnp.broadcast_to(speed_ref[...], shape) * volume
    weight_ref[1] = jnp.broadcast_to(visc_ref[...], shape) * volume
    weight_ref[2] = jnp.where(lane_ids() < jnp.broadcast_to(count_ref[...], shape), 1.0, 0.0)
    for face in range(4):
        entry = jnp.broadcast_to(conn_ref[pl.ds(face, 1), :], shape)
        entry_ref[face] = entry
        ghost = entry - cells
        ghost = jnp.where(
            ghost < 2 * slots,
            jnp.bitwise_xor(ghost, row_swap),
            jnp.where(ghost < 4 * slots, jnp.bitwise_xor(ghost, col_swap), ghost),
        )
        for m in range(groups):
            ghost_ref[face, pl.ds(m * sublanes, sublanes), :] = jnp.bitwise_and(
                ghost + m * slots, lanes - 1
            )
        for j in range(fields):
            splat_ref[pl.ds((face * fields + j) * fields, fields), :] = jnp.broadcast_to(
                jac_ref[face, :, pl.ds(j, 1)], (fields, lanes)
            )


def stage_kernel(
    stage,
    chunk,
    weight_ref,
    entry_ref,
    ghost_ref,
    splat_ref,
    send_table_ref,
    q_ref,
    *refs,
):
    refs = list(refs)
    state_ref = q_ref if stage == 0 else refs.pop(0)
    acc_ref = q_ref if stage == 0 else refs.pop(0)
    recv_refs = [refs.pop(0) for _ in range(4)]
    fields, vectors, cells = q_ref.shape
    groups = vectors // sublanes
    slots = lanes // groups
    group = lane_ids() // slots

    def tall(value):
        return value if chunk == 1 else jnp.concatenate([value] * chunk, axis=0)

    advect = tall(weight_ref[0])
    diffuse = tall(weight_ref[1])
    last = stage == 3
    kept_coef = time_step / 6.0 if stage in (0, 3) else time_step / 3.0
    next_coef = (0.5 * time_step, 0.5 * time_step, time_step, None)[stage]
    if last:
        advanced_ref, gram_ref = refs
        live = tall(weight_ref[2]) > 0.5
    else:
        next_ref, next_acc_ref, *out_refs = refs
    states = []
    zero = jnp.zeros((sublanes, lanes), jnp.float32)
    for start in range(0, groups, chunk):
        rows = pl.ds(start * sublanes, chunk * sublanes)
        own = [state_ref[f, rows, :] for f in range(fields)]
        ghosts = []
        for f in range(fields):
            parts = []
            for m in range(start, start + chunk):
                block = zero
                for b in range(4):
                    block = jnp.where(group == (m + b) % groups, recv_refs[b][f], block)
                parts.append(block)
            ghosts.append(jnp.concatenate(parts, axis=0))
        advection = [None] * fields
        diffusion = [-4.0 * own[f] for f in range(fields)]
        for face in range(4):
            entry = tall(entry_ref[face])
            outside = entry >= cells
            inside_index = jnp.bitwise_and(entry, lanes - 1)
            outside_index = ghost_ref[face, rows, :]
            for j in range(fields):
                near = jnp.where(
                    outside,
                    lane_take(ghosts[j], outside_index),
                    lane_take(own[j], inside_index),
                )
                diffusion[j] = diffusion[j] + near
                for i in range(fields):
                    at = (face * fields + j) * fields + i
                    term = splat_ref[pl.ds(at, 1), :] * near
                    advection[i] = term if advection[i] is None else advection[i] + term
        following = []
        for f in range(fields):
            slope = advect * advection[f] + diffuse * diffusion[f]
            kept = acc_ref[f, rows, :] + kept_coef * slope
            if last:
                advanced_ref[f, rows, :] = jnp.where(live, kept, 0.0)
            else:
                next_acc_ref[f, rows, :] = kept
                after = q_ref[f, rows, :] + next_coef * slope
                next_ref[f, rows, :] = after
                following.append(after)
        if not last:
            for m in range(chunk):
                states.append([x[m * sublanes : (m + 1) * sublanes] for x in following])
    if not last:
        pack(states, send_table_ref, out_refs, groups, slots)
        return
    half = vectors // 2
    wide = jnp.concatenate([advanced_ref[f] for f in range(fields)], axis=1)
    gram = lax.dot_general(
        wide,
        jnp.concatenate([wide, jnp.zeros_like(wide)], axis=0),
        (((1,), (1,)), ((), ())),
        precision=HIGHEST,
        preferred_element_type=jnp.float32,
    )
    gram_ref[...] = gram[:half] + pltpu.roll(gram[half:], vectors, 1)


def factor_kernel(scale, gram_ref, advanced_ref, basis_ref, factor_ref):
    fields, vectors, cells = advanced_ref.shape
    half = vectors // 2
    folded = gram_ref[...] * scale
    turned = pltpu.roll(folded, vectors, 1)
    work = jnp.concatenate([folded, turned], axis=0)
    row = lax.broadcasted_iota(jnp.int32, (vectors, lanes), 0)
    lane = lax.broadcasted_iota(jnp.int32, (vectors, lanes), 1)
    work = jnp.where(lane < vectors, work, jnp.where(lane == row + vectors, 1.0, 0.0))
    blocks = [work[b * sublanes : (b + 1) * sublanes] for b in range(vectors // sublanes)]
    sub = lax.broadcasted_iota(jnp.int32, (sublanes, lanes), 0)
    scales = []
    for b in range(len(blocks)):
        start = b * sublanes
        count = len(blocks) - b
        columns = [
            [
                jnp.broadcast_to(blocks[c][:, start + k : start + k + 1], (sublanes, lanes))
                for c in range(b, len(blocks))
            ]
            for k in range(sublanes)
        ]
        for k in range(sublanes):
            pivot = jnp.broadcast_to(columns[k][0][k : k + 1], (sublanes, lanes))
            scales.append(pivot)
            inverse = 1.0 / pivot
            row_k = jnp.broadcast_to(blocks[b][k : k + 1], (sublanes, lanes)) * inverse
            later = [
                jnp.broadcast_to(columns[n][0][k : k + 1], (sublanes, lanes)) * inverse
                for n in range(k + 1, sublanes)
            ]
            for c in range(count):
                ratio = columns[k][c]
                if c == 0:
                    ratio = jnp.where(sub > k, ratio, 0.0)
                blocks[b + c] = blocks[b + c] - ratio * row_k
                for n in range(k + 1, sublanes):
                    columns[n][c] = columns[n][c] - ratio * later[n - k - 1]
    for b in range(len(blocks)):
        pivots = scales[b * sublanes]
        for k in range(1, sublanes):
            pivots = jnp.where(sub == k, scales[b * sublanes + k], pivots)
        blocks[b] = blocks[b] * lax.rsqrt(pivots)
    done = jnp.concatenate(blocks, axis=0)
    factor_ref[...] = jnp.where(lane >= row, done, 0.0)[:, :vectors]
    inverse_lower = pltpu.roll(done, vectors, 1)[:, :vectors]
    for f in range(fields):
        basis_ref[f] = jnp.dot(
            inverse_lower,
            advanced_ref[f],
            precision=HIGHEST,
            preferred_element_type=jnp.float32,
        )


def summed(value, rows, cols):
    steps = [(1, 0)]
    step = 2
    while step < rows:
        steps.append((step + 1, 0))
        step *= 2
    step = 1
    while step < cols:
        steps.append((1, step))
        step *= 2
    for across, along in steps:
        pairs = [
            (i * cols + j, (i ^ across) * cols + (j ^ along))
            for i in range(rows)
            for j in range(cols)
        ]
        value = value + lax.ppermute(value, ("gx", "gy"), pairs)
    return value


def shards(
    mesh_shape,
    test_vectors,
    face_jacobians,
    wave_speed,
    viscosity,
    inverse_volume,
    connectivity,
    send_rows,
    cell_count,
):
    rows, cols = mesh_shape
    fields, vectors, cells = test_vectors.shape
    slots = send_rows.shape[1]
    groups = vectors // sublanes
    assert cells == lanes and groups * slots == lanes and 2 * vectors == lanes
    vmem = pl.BlockSpec(memory_space=pltpu.VMEM)
    speed = wave_speed.reshape(1, cells)
    visc = viscosity.reshape(1, cells)
    volume = inverse_volume.reshape(1, cells)
    state = jax.ShapeDtypeStruct(test_vectors.shape, jnp.float32)
    block = jax.ShapeDtypeStruct((fields, sublanes, lanes), jnp.float32)
    tables = [
        jax.ShapeDtypeStruct((3, sublanes, lanes), jnp.float32),
        jax.ShapeDtypeStruct((4, sublanes, lanes), jnp.int32),
        jax.ShapeDtypeStruct((4, vectors, lanes), jnp.int32),
        jax.ShapeDtypeStruct((4 * fields * fields, lanes), jnp.float32),
    ]
    params = pltpu.CompilerParams(vmem_limit_bytes=16 * 1024 * 1024)
    pairs = matchings(rows, cols)

    def exchange(sent):
        got = [None] * 4
        for which in (0, 3, 2, 1):
            got[which] = lax.ppermute(sent[which], ("gx", "gy"), pairs[which])
        return got

    send_table, *sent = pl.pallas_call(
        prepare_kernel,
        out_shape=[jax.ShapeDtypeStruct((vectors, lanes), jnp.int32)] + [block] * 4,
        in_specs=[vmem] * 2,
        out_specs=[vmem] * 5,
        compiler_params=params,
        name="prepare",
    )(send_rows, test_vectors)
    tables = pl.pallas_call(
        functools.partial(tables_kernel, slots),
        out_shape=tables,
        in_specs=[vmem] * 6,
        out_specs=[vmem] * 4,
        compiler_params=params,
        name="tables",
    )(cell_count.reshape(1, 1), face_jacobians, connectivity, speed, visc, volume)
    held = []
    for stage in range(4):
        got = exchange(sent)
        last = stage == 3
        gram_shape = jax.ShapeDtypeStruct((vectors // 2, lanes), jnp.float32)
        result = pl.pallas_call(
            functools.partial(stage_kernel, stage, 1),
            out_shape=[state, gram_shape] if last else [state, state] + [block] * 4,
            in_specs=[vmem] * (6 + len(held) + 4),
            out_specs=[vmem] * (2 if last else 6),
            compiler_params=params,
            name="stage",
        )(*tables, send_table, test_vectors, *held, *got)
        held, sent = result[:2], result[2:]
    advanced, gram = held
    gram = summed(gram, rows, cols)
    scale = 1.0 / float(fields * cells * rows * cols)
    return pl.pallas_call(
        functools.partial(factor_kernel, scale),
        out_shape=[state, jax.ShapeDtypeStruct((vectors, vectors), jnp.float32)],
        in_specs=[vmem] * 2,
        out_specs=[vmem] * 2,
        compiler_params=params,
        name="factor",
    )(gram, advanced)


def solution(mesh):
    placed = (
        P(None, None, ("gx", "gy")),
        P(),
        P(("gx", "gy")),
        P(("gx", "gy")),
        P(("gx", "gy")),
        P(None, ("gx", "gy")),
        P(None, ("gx", "gy")),
        P(("gx", "gy")),
    )
    return jax.shard_map(
        functools.partial(shards, (mesh.shape["gx"], mesh.shape["gy"])),
        mesh=mesh,
        in_specs=placed,
        out_specs=(P(None, None, ("gx", "gy")), P()),
        check_vma=False,
    )
```

```python
import functools

import jax
import jax.numpy as jnp
from jax import lax
from jax.experimental import pallas as pl
from jax.experimental.pallas import tpu as pltpu
from jax.sharding import PartitionSpec as P

time_step = 0.4
lanes = 128
sublanes = 8
HIGHEST = lax.Precision.HIGHEST


def partner(index, count, odd):
    other = index + 1 if index % 2 == odd else index - 1
    return other if 0 <= other < count else None


def matchings(rows, cols):
    row_even, row_odd, col_even, col_odd = [], [], [], []
    for i in range(rows):
        for j in range(cols):
            here = i * cols + j
            row_even.append((here, (i ^ 1) * cols + j))
            col_even.append((here, i * cols + (j ^ 1)))
            up = partner(i, rows, 1)
            row_odd.append((here, (rows - 1 - i if up is None else up) * cols + j))
            across = partner(j, cols, 1)
            col_odd.append((here, (i ^ 1) * cols + j if across is None else i * cols + across))
    return row_even, row_odd, col_even, col_odd


def lane_take(values, index):
    return jnp.take_along_axis(values, index, axis=1, mode="promise_in_bounds")


def lane_ids():
    return lax.broadcasted_iota(jnp.int32, (sublanes, lanes), 1)


def pack(states, group, send_table_ref, out_refs, groups):
    fields = len(states[0])
    packed = [[None] * fields for _ in range(4)]
    for m in range(groups):
        index = send_table_ref[pl.ds(m * sublanes, sublanes), :]
        for f in range(fields):
            taken = lane_take(states[m][f], index)
            for b in range(4):
                before = packed[b][f]
                packed[b][f] = (
                    taken
                    if before is None
                    else jnp.where(group == (m + b) % groups, taken, before)
                )
    for b in range(4):
        for f in range(fields):
            out_refs[b][f] = packed[b][f]


def groups_kernel(slots, group_ref):
    group_ref[...] = lane_ids() // slots


def prepare_kernel(group_ref, q_ref, send_ref, send_table_ref, *out_refs):
    fields, vectors, _ = q_ref.shape
    slots = send_ref.shape[1]
    groups = lanes // slots
    shape = (sublanes, lanes)
    group = group_ref[...]
    row_even = lax.axis_index("gx") % 2 == 0
    col_even = lax.axis_index("gy") % 2 == 0
    sends = jnp.concatenate(
        [send_ref[...], jnp.zeros((4, lanes - slots), jnp.int32)], axis=1
    )
    spread = [jnp.broadcast_to(sends[b : b + 1], shape) for b in range(4)]
    ordered = [
        jnp.where(row_even, spread[1], spread[0]),
        jnp.where(row_even, spread[0], spread[1]),
        jnp.where(col_even, spread[3], spread[2]),
        jnp.where(col_even, spread[2], spread[3]),
    ]
    base = ordered[0]
    for b in range(1, 4):
        base = jnp.where(group == b, pltpu.roll(ordered[b], b * slots, 1), base)
    for m in range(groups):
        send_table_ref[pl.ds(m * sublanes, sublanes), :] = (
            pltpu.roll(base, m * slots, 1) if m else base
        )
    states = [
        [q_ref[f, pl.ds(m * sublanes, sublanes), :] for f in range(fields)] for m in range(groups)
    ]
    pack(states, group, send_table_ref, out_refs, groups)


def tables_kernel(
    slots,
    count_ref,
    jac_ref,
    conn_ref,
    speed_ref,
    visc_ref,
    volume_ref,
    centre_ref,
    inside_ref,
    outside_ref,
    own_coef_ref,
    ghost_coef_ref,
):
    cells = conn_ref.shape[1]
    fields = jac_ref.shape[0]
    groups = lanes // slots
    shape = (sublanes, lanes)
    row_swap = jnp.where(lax.axis_index("gx") % 2 == 0, slots, 0)
    col_swap = jnp.where(lax.axis_index("gy") % 2 == 0, slots, 0)
    volume = jnp.broadcast_to(volume_ref[...], shape)
    advect = -0.5 * jnp.broadcast_to(speed_ref[...], shape) * volume
    diffuse = jnp.broadcast_to(visc_ref[...], shape) * volume
    centre_ref[0] = -4.0 * diffuse
    centre_ref[1] = jnp.where(lane_ids() < jnp.broadcast_to(count_ref[...], shape), 1.0, 0.0)
    sub = lax.broadcasted_iota(jnp.int32, shape, 0)
    for face in range(4):
        entry = jnp.broadcast_to(conn_ref[pl.ds(face, 1), :], shape)
        owned = entry < cells
        far = entry >= cells + 4 * slots
        inside_ref[face] = jnp.bitwise_and(entry, lanes - 1)
        ghost = entry - cells
        ghost = jnp.where(
            ghost < 2 * slots,
            jnp.bitwise_xor(ghost, row_swap),
            jnp.where(ghost < 4 * slots, jnp.bitwise_xor(ghost, col_swap), ghost),
        )
        for m in range(groups):
            outside_ref[face, pl.ds(m * sublanes, sublanes), :] = jnp.bitwise_and(
                ghost + m * slots, lanes - 1
            )
        for j in range(fields):
            rows = pl.ds((face * fields + j) * fields, fields)
            jacobian = jnp.broadcast_to(jac_ref[:, face, pl.ds(j, 1)], (fields, lanes))
            coef = jacobian * advect[:fields] + jnp.where(sub == j, diffuse, 0.0)[:fields]
            own_coef_ref[rows, :] = jnp.where(owned[:fields], coef, 0.0)
            ghost_coef_ref[rows, :] = jnp.where((owned | far)[:fields], 0.0, coef)


def coefficients(stage):
    kept = time_step / 6.0 if stage in (0, 3) else time_step / 3.0
    return kept, (0.5 * time_step, 0.5 * time_step, time_step, None)[stage]


def neighbours(near, coef_ref, totals, face):
    fields = len(near)
    for j in range(fields):
        for i in range(fields):
            at = (face * fields + j) * fields + i
            term = coef_ref[pl.ds(at, 1), :] * near[j]
            totals[i] = term if totals[i] is None else totals[i] + term


def own_kernel(stage, centre_ref, inside_ref, coef_ref, q_ref, *refs):
    refs = list(refs)
    state_ref = q_ref if stage == 0 else refs.pop(0)
    acc_ref = q_ref if stage == 0 else refs.pop(0)
    kept_coef, next_coef = coefficients(stage)
    fields, vectors, _ = q_ref.shape
    for start in range(0, vectors, sublanes):
        rows = pl.ds(start, sublanes)
        own = [state_ref[f, rows, :] for f in range(fields)]
        totals = [centre_ref[0] * own[f] for f in range(fields)]
        for face in range(4):
            near = [lane_take(own[f], inside_ref[face]) for f in range(fields)]
            neighbours(near, coef_ref, totals, face)
        for f in range(fields):
            refs[0][f, rows, :] = acc_ref[f, rows, :] + kept_coef * totals[f]
            if next_coef is not None:
                refs[1][f, rows, :] = q_ref[f, rows, :] + next_coef * totals[f]


def ghost_kernel(stage, outside_ref, coef_ref, centre_ref, group_ref, send_table_ref, *refs):
    refs = list(refs)
    last = stage == 3
    part_refs = [refs.pop(0) for _ in range(1 if last else 2)]
    recv_refs = [refs.pop(0) for _ in range(4)]
    kept_coef, next_coef = coefficients(stage)
    fields, vectors, cells = part_refs[0].shape
    groups = vectors // sublanes
    group = group_ref[...]
    states = []
    for m in range(groups):
        rows = pl.ds(m * sublanes, sublanes)
        ghosts = []
        for f in range(fields):
            block = recv_refs[0][f]
            for b in range(1, 4):
                block = jnp.where(group == (m + b) % groups, recv_refs[b][f], block)
            ghosts.append(block)
        totals = [None] * fields
        for face in range(4):
            near = [lane_take(ghosts[f], outside_ref[face, rows, :]) for f in range(fields)]
            neighbours(near, coef_ref, totals, face)
        following = []
        for f in range(fields):
            kept = part_refs[0][f, rows, :] + kept_coef * totals[f]
            refs[0][f, rows, :] = kept * centre_ref[1] if last else kept
            if not last:
                after = part_refs[1][f, rows, :] + next_coef * totals[f]
                refs[1][f, rows, :] = after
                following.append(after)
        states.append(following)
    if not last:
        pack(states, group, send_table_ref, refs[2:], groups)
        return
    half = vectors // 2
    wide = jnp.concatenate([refs[0][f] for f in range(fields)], axis=1)
    gram = lax.dot_general(
        wide,
        jnp.concatenate([wide, jnp.zeros_like(wide)], axis=0),
        (((1,), (1,)), ((), ())),
        precision=HIGHEST,
        preferred_element_type=jnp.float32,
    )
    refs[1][...] = gram[:half] + pltpu.roll(gram[half:], vectors, 1)


def factor_kernel(scale, gram_ref, advanced_ref, basis_ref, factor_ref):
    fields, vectors, cells = advanced_ref.shape
    half = vectors // 2
    folded = gram_ref[...] * scale
    turned = pltpu.roll(folded, vectors, 1)
    work = jnp.concatenate([folded, turned], axis=0)
    row = lax.broadcasted_iota(jnp.int32, (vectors, lanes), 0)
    lane = lax.broadcasted_iota(jnp.int32, (vectors, lanes), 1)
    work = jnp.where(lane < vectors, work, jnp.where(lane == row + vectors, 1.0, 0.0))
    blocks = [work[b * sublanes : (b + 1) * sublanes] for b in range(vectors // sublanes)]
    sub = lax.broadcasted_iota(jnp.int32, (sublanes, lanes), 0)
    scales = []
    for b in range(len(blocks)):
        start = b * sublanes
        count = len(blocks) - b
        columns = [
            [
                jnp.broadcast_to(blocks[c][:, start + k : start + k + 1], (sublanes, lanes))
                for c in range(b, len(blocks))
            ]
            for k in range(sublanes)
        ]
        for k in range(sublanes):
            pivot = jnp.broadcast_to(columns[k][0][k : k + 1], (sublanes, lanes))
            scales.append(pivot)
            inverse = 1.0 / pivot
            row_k = jnp.broadcast_to(blocks[b][k : k + 1], (sublanes, lanes)) * inverse
            later = [
                jnp.broadcast_to(columns[n][0][k : k + 1], (sublanes, lanes)) * inverse
                for n in range(k + 1, sublanes)
            ]
            for c in range(count):
                ratio = columns[k][c]
                if c == 0:
                    ratio = jnp.where(sub > k, ratio, 0.0)
                blocks[b + c] = blocks[b + c] - ratio * row_k
                for n in range(k + 1, sublanes):
                    columns[n][c] = columns[n][c] - ratio * later[n - k - 1]
    for b in range(len(blocks)):
        pivots = scales[b * sublanes]
        for k in range(1, sublanes):
            pivots = jnp.where(sub == k, scales[b * sublanes + k], pivots)
        blocks[b] = blocks[b] * lax.rsqrt(pivots)
    done = jnp.concatenate(blocks, axis=0)
    factor_ref[...] = jnp.where(lane >= row, done, 0.0)[:, :vectors]
    inverse_lower = pltpu.roll(done, vectors, 1)[:, :vectors]
    for f in range(fields):
        basis_ref[f] = jnp.dot(
            inverse_lower,
            advanced_ref[f],
            precision=HIGHEST,
            preferred_element_type=jnp.float32,
        )


def summed(value, rows, cols):
    steps = [(1, 0)]
    step = 2
    while step < rows:
        steps.append((step + 1, 0))
        step *= 2
    step = 1
    while step < cols:
        steps.append((1, step))
        step *= 2
    for across, along in steps:
        pairs = [
            (i * cols + j, (i ^ across) * cols + (j ^ along))
            for i in range(rows)
            for j in range(cols)
        ]
        value = value + lax.ppermute(value, ("gx", "gy"), pairs)
    return value


def shards(
    mesh_shape,
    test_vectors,
    face_jacobians,
    wave_speed,
    viscosity,
    inverse_volume,
    connectivity,
    send_rows,
    cell_count,
):
    rows, cols = mesh_shape
    fields, vectors, cells = test_vectors.shape
    slots = send_rows.shape[1]
    groups = vectors // sublanes
    assert cells == lanes and groups * slots == lanes and 2 * vectors == lanes
    vmem = pl.BlockSpec(memory_space=pltpu.VMEM)
    speed = wave_speed.reshape(1, cells)
    visc = viscosity.reshape(1, cells)
    volume = inverse_volume.reshape(1, cells)
    state = jax.ShapeDtypeStruct(test_vectors.shape, jnp.float32)
    block = jax.ShapeDtypeStruct((fields, sublanes, lanes), jnp.float32)
    coefs = jax.ShapeDtypeStruct((4 * fields * fields, lanes), jnp.float32)
    tables = [
        jax.ShapeDtypeStruct((2, sublanes, lanes), jnp.float32),
        jax.ShapeDtypeStruct((4, sublanes, lanes), jnp.int32),
        jax.ShapeDtypeStruct((4, vectors, lanes), jnp.int32),
        coefs,
        coefs,
    ]
    params = pltpu.CompilerParams(vmem_limit_bytes=16 * 1024 * 1024)
    pairs = matchings(rows, cols)

    def exchange(sent):
        got = [None] * 4
        for which in (0, 3, 2, 1):
            got[which] = lax.ppermute(sent[which], ("gx", "gy"), pairs[which])
        return got

    ahead = pl.CostEstimate(flops=4 * 10**9, bytes_accessed=8 * 10**6, transcendentals=0)
    tile = jax.ShapeDtypeStruct((sublanes, lanes), jnp.int32)
    group = pl.pallas_call(
        functools.partial(groups_kernel, slots),
        out_shape=tile,
        out_specs=vmem,
        compiler_params=params,
        cost_estimate=ahead,
        name="groups",
    )()
    send_table, *sent = pl.pallas_call(
        prepare_kernel,
        out_shape=[jax.ShapeDtypeStruct((vectors, lanes), jnp.int32)] + [block] * 4,
        in_specs=[vmem] * 3,
        out_specs=[vmem] * 5,
        compiler_params=params,
        name="prepare",
    )(group, test_vectors, send_rows)
    centre, inside, outside, own_coef, ghost_coef = pl.pallas_call(
        functools.partial(tables_kernel, slots),
        out_shape=tables,
        in_specs=[vmem] * 6,
        out_specs=[vmem] * 5,
        compiler_params=params,
        name="tables",
    )(
        cell_count.reshape(1, 1),
        face_jacobians.transpose(1, 0, 2),
        connectivity,
        speed,
        visc,
        volume,
    )
    held = []
    for stage in range(4):
        last = stage == 3
        got = exchange(sent)
        partial = pl.pallas_call(
            functools.partial(own_kernel, stage),
            out_shape=[state] * (1 if last else 2),
            in_specs=[vmem] * (4 + len(held)),
            out_specs=[vmem] * (1 if last else 2),
            compiler_params=params,
            name="own",
        )(centre, inside, own_coef, test_vectors, *held)
        gram_shape = jax.ShapeDtypeStruct((vectors // 2, lanes), jnp.float32)
        result = pl.pallas_call(
            functools.partial(ghost_kernel, stage),
            out_shape=[state, gram_shape] if last else [state, state] + [block] * 4,
            in_specs=[vmem] * (5 + len(partial) + 4),
            out_specs=[vmem] * (2 if last else 6),
            compiler_params=params,
            name="ghost",
        )(outside, ghost_coef, centre, group, send_table, *partial, *got)
        held, sent = result[1::-1], result[2:]
    gram, advanced = held
    gram = summed(gram, rows, cols)
    scale = 1.0 / float(fields * cells * rows * cols)
    return pl.pallas_call(
        functools.partial(factor_kernel, scale),
        out_shape=[state, jax.ShapeDtypeStruct((vectors, vectors), jnp.float32)],
        in_specs=[vmem] * 2,
        out_specs=[vmem] * 2,
        compiler_params=params,
        name="factor",
    )(gram, advanced)


def solution(mesh):
    placed = (
        P(None, None, ("gx", "gy")),
        P(),
        P(("gx", "gy")),
        P(("gx", "gy")),
        P(("gx", "gy")),
        P(None, ("gx", "gy")),
        P(None, ("gx", "gy")),
        P(("gx", "gy")),
    )
    return jax.shard_map(
        functools.partial(shards, (mesh.shape["gx"], mesh.shape["gy"])),
        mesh=mesh,
        in_specs=placed,
        out_specs=(P(None, None, ("gx", "gy")), P()),
        check_vma=False,
    )
```

```python
import functools

import jax
import jax.numpy as jnp
from jax import lax
from jax.experimental import pallas as pl
from jax.experimental.pallas import tpu as pltpu
from jax.sharding import PartitionSpec as P

time_step = 0.4
arrival = (1, 2, 3, 0)
lanes = 128
sublanes = 8
HIGHEST = lax.Precision.HIGHEST


def partner(index, count, odd):
    other = index + 1 if index % 2 == odd else index - 1
    return other if 0 <= other < count else None


def matchings(rows, cols):
    row_even, row_odd, col_even, col_odd = [], [], [], []
    for i in range(rows):
        for j in range(cols):
            here = i * cols + j
            row_even.append((here, (i ^ 1) * cols + j))
            col_even.append((here, i * cols + (j ^ 1)))
            up = partner(i, rows, 1)
            row_odd.append((here, (rows - 1 - i if up is None else up) * cols + j))
            across = partner(j, cols, 1)
            col_odd.append((here, (i ^ 1) * cols + j if across is None else i * cols + across))
    return row_even, row_odd, col_even, col_odd


def lane_take(values, index):
    return jnp.take_along_axis(values, index, axis=1, mode="promise_in_bounds")


def lane_ids():
    return lax.broadcasted_iota(jnp.int32, (sublanes, lanes), 1)


def pack(states, group, send_table_ref, out_refs, groups):
    fields = len(states[0])
    packed = [[None] * fields for _ in range(4)]
    for m in range(groups):
        index = send_table_ref[pl.ds(m * sublanes, sublanes), :]
        for f in range(fields):
            taken = lane_take(states[m][f], index)
            for b in range(4):
                before = packed[b][f]
                packed[b][f] = (
                    taken
                    if before is None
                    else jnp.where(group == (m + b) % groups, taken, before)
                )
    for b in range(4):
        for f in range(fields):
            out_refs[b][f] = packed[b][f]


def groups_kernel(slots, group_ref):
    group_ref[...] = lane_ids() // slots


def prepare_kernel(group_ref, q_ref, send_ref, send_table_ref, *out_refs):
    fields, vectors, _ = q_ref.shape
    slots = send_ref.shape[1]
    groups = lanes // slots
    shape = (sublanes, lanes)
    group = group_ref[...]
    row_even = lax.axis_index("gx") % 2 == 0
    col_even = lax.axis_index("gy") % 2 == 0
    sends = jnp.concatenate(
        [send_ref[...], jnp.zeros((4, lanes - slots), jnp.int32)], axis=1
    )
    spread = [jnp.broadcast_to(sends[b : b + 1], shape) for b in range(4)]
    ordered = [
        jnp.where(row_even, spread[1], spread[0]),
        jnp.where(row_even, spread[0], spread[1]),
        jnp.where(col_even, spread[3], spread[2]),
        jnp.where(col_even, spread[2], spread[3]),
    ]
    base = ordered[0]
    for b in range(1, 4):
        base = jnp.where(group == b, pltpu.roll(ordered[b], b * slots, 1), base)
    for m in range(groups):
        send_table_ref[pl.ds(m * sublanes, sublanes), :] = (
            pltpu.roll(base, m * slots, 1) if m else base
        )
    states = [
        [q_ref[f, pl.ds(m * sublanes, sublanes), :] for f in range(fields)] for m in range(groups)
    ]
    pack(states, group, send_table_ref, out_refs, groups)


def tables_kernel(
    slots,
    count_ref,
    jac_ref,
    conn_ref,
    speed_ref,
    visc_ref,
    volume_ref,
    centre_ref,
    inside_ref,
    outside_ref,
    own_coef_ref,
    ghost_coef_ref,
):
    cells = conn_ref.shape[1]
    fields = jac_ref.shape[0]
    groups = lanes // slots
    shape = (sublanes, lanes)
    row_swap = jnp.where(lax.axis_index("gx") % 2 == 0, slots, 0)
    col_swap = jnp.where(lax.axis_index("gy") % 2 == 0, slots, 0)
    volume = jnp.broadcast_to(volume_ref[...], shape)
    advect = -0.5 * jnp.broadcast_to(speed_ref[...], shape) * volume
    diffuse = jnp.broadcast_to(visc_ref[...], shape) * volume
    centre_ref[0] = -4.0 * diffuse
    centre_ref[1] = jnp.where(lane_ids() < jnp.broadcast_to(count_ref[...], shape), 1.0, 0.0)
    sub = lax.broadcasted_iota(jnp.int32, shape, 0)
    for face in range(4):
        entry = jnp.broadcast_to(conn_ref[pl.ds(face, 1), :], shape)
        owned = entry < cells
        far = entry >= cells + 4 * slots
        inside_ref[face] = jnp.bitwise_and(entry, lanes - 1)
        ghost = entry - cells
        ghost = jnp.where(
            ghost < 2 * slots,
            jnp.bitwise_xor(ghost, row_swap),
            jnp.where(ghost < 4 * slots, jnp.bitwise_xor(ghost, col_swap), ghost),
        )
        for m in range(groups):
            outside_ref[face, pl.ds(m * sublanes, sublanes), :] = jnp.bitwise_and(
                ghost + m * slots, lanes - 1
            )
        for j in range(fields):
            rows = pl.ds((face * fields + j) * fields, fields)
            jacobian = jnp.broadcast_to(jac_ref[:, face, pl.ds(j, 1)], (fields, lanes))
            coef = jacobian * advect[:fields] + jnp.where(sub == j, diffuse, 0.0)[:fields]
            own_coef_ref[rows, :] = jnp.where(owned[:fields], coef, 0.0)
            ghost_coef_ref[rows, :] = jnp.where((owned | far)[:fields], 0.0, coef)


def coefficients(stage):
    kept = time_step / 6.0 if stage in (0, 3) else time_step / 3.0
    return kept, (0.5 * time_step, 0.5 * time_step, time_step, None)[stage]


def neighbours(near, coef_ref, totals, face):
    fields = len(near)
    for j in range(fields):
        for i in range(fields):
            at = (face * fields + j) * fields + i
            term = coef_ref[pl.ds(at, 1), :] * near[j]
            totals[i] = term if totals[i] is None else totals[i] + term


def own_kernel(stage, centre_ref, inside_ref, coef_ref, q_ref, *refs):
    refs = list(refs)
    state_ref = q_ref if stage == 0 else refs.pop(0)
    acc_ref = q_ref if stage == 0 else refs.pop(0)
    kept_coef, next_coef = coefficients(stage)
    fields, vectors, _ = q_ref.shape
    for start in range(0, vectors, sublanes):
        rows = pl.ds(start, sublanes)
        own = [state_ref[f, rows, :] for f in range(fields)]
        totals = [centre_ref[0] * own[f] for f in range(fields)]
        for face in range(4):
            near = [lane_take(own[f], inside_ref[face]) for f in range(fields)]
            neighbours(near, coef_ref, totals, face)
        for f in range(fields):
            refs[0][f, rows, :] = acc_ref[f, rows, :] + kept_coef * totals[f]
            if next_coef is not None:
                refs[1][f, rows, :] = q_ref[f, rows, :] + next_coef * totals[f]


def ghost_kernel(stage, outside_ref, coef_ref, centre_ref, group_ref, send_table_ref, *refs):
    refs = list(refs)
    last = stage == 3
    part_refs = [refs.pop(0) for _ in range(1 if last else 2)]
    recv_refs = dict(zip(arrival, (refs.pop(0) for _ in range(4))))
    kept_coef, next_coef = coefficients(stage)
    fields, vectors, cells = part_refs[0].shape
    groups = vectors // sublanes
    group = group_ref[...]
    states = []
    for m in range(groups):
        rows = pl.ds(m * sublanes, sublanes)
        ghosts = []
        for f in range(fields):
            block = recv_refs[0][f]
            for b in range(1, 4):
                block = jnp.where(group == (m + b) % groups, recv_refs[b][f], block)
            ghosts.append(block)
        totals = [None] * fields
        for face in range(4):
            near = [lane_take(ghosts[f], outside_ref[face, rows, :]) for f in range(fields)]
            neighbours(near, coef_ref, totals, face)
        following = []
        for f in range(fields):
            kept = part_refs[0][f, rows, :] + kept_coef * totals[f]
            refs[0][f, rows, :] = kept * centre_ref[1] if last else kept
            if not last:
                after = part_refs[1][f, rows, :] + next_coef * totals[f]
                refs[1][f, rows, :] = after
                following.append(after)
        states.append(following)
    if not last:
        pack(states, group, send_table_ref, refs[2:], groups)
        return
    half = vectors // 2
    wide = jnp.concatenate([refs[0][f] for f in range(fields)], axis=1)
    gram = lax.dot_general(
        wide,
        jnp.concatenate([wide, jnp.zeros_like(wide)], axis=0),
        (((1,), (1,)), ((), ())),
        precision=HIGHEST,
        preferred_element_type=jnp.float32,
    )
    refs[1][...] = gram[:half] + pltpu.roll(gram[half:], vectors, 1)


def factor_kernel(scale, gram_ref, advanced_ref, basis_ref, factor_ref):
    fields, vectors, cells = advanced_ref.shape
    half = vectors // 2
    folded = gram_ref[...] * scale
    turned = pltpu.roll(folded, vectors, 1)
    work = jnp.concatenate([folded, turned], axis=0)
    row = lax.broadcasted_iota(jnp.int32, (vectors, lanes), 0)
    lane = lax.broadcasted_iota(jnp.int32, (vectors, lanes), 1)
    work = jnp.where(lane < vectors, work, jnp.where(lane == row + vectors, 1.0, 0.0))
    blocks = [work[b * sublanes : (b + 1) * sublanes] for b in range(vectors // sublanes)]
    sub = lax.broadcasted_iota(jnp.int32, (sublanes, lanes), 0)
    scales = []
    for b in range(len(blocks)):
        start = b * sublanes
        count = len(blocks) - b
        columns = [
            [
                jnp.broadcast_to(blocks[c][:, start + k : start + k + 1], (sublanes, lanes))
                for c in range(b, len(blocks))
            ]
            for k in range(sublanes)
        ]
        for k in range(sublanes):
            pivot = jnp.broadcast_to(columns[k][0][k : k + 1], (sublanes, lanes))
            scales.append(pivot)
            inverse = 1.0 / pivot
            row_k = jnp.broadcast_to(blocks[b][k : k + 1], (sublanes, lanes)) * inverse
            later = [
                jnp.broadcast_to(columns[n][0][k : k + 1], (sublanes, lanes)) * inverse
                for n in range(k + 1, sublanes)
            ]
            for c in range(count):
                ratio = columns[k][c]
                if c == 0:
                    ratio = jnp.where(sub > k, ratio, 0.0)
                blocks[b + c] = blocks[b + c] - ratio * row_k
                for n in range(k + 1, sublanes):
                    columns[n][c] = columns[n][c] - ratio * later[n - k - 1]
    for b in range(len(blocks)):
        pivots = scales[b * sublanes]
        for k in range(1, sublanes):
            pivots = jnp.where(sub == k, scales[b * sublanes + k], pivots)
        blocks[b] = blocks[b] * lax.rsqrt(pivots)
    done = jnp.concatenate(blocks, axis=0)
    factor_ref[...] = jnp.where(lane >= row, done, 0.0)[:, :vectors]
    inverse_lower = pltpu.roll(done, vectors, 1)[:, :vectors]
    for f in range(fields):
        basis_ref[f] = jnp.dot(
            inverse_lower,
            advanced_ref[f],
            precision=HIGHEST,
            preferred_element_type=jnp.float32,
        )


def summed(value, rows, cols):
    steps = [(1, 0)]
    step = 2
    while step < rows:
        steps.append((step + 1, 0))
        step *= 2
    step = 1
    while step < cols:
        steps.append((1, step))
        step *= 2
    for across, along in steps:
        pairs = [
            (i * cols + j, (i ^ across) * cols + (j ^ along))
            for i in range(rows)
            for j in range(cols)
        ]
        value = value + lax.ppermute(value, ("gx", "gy"), pairs)
    return value


def shards(
    mesh_shape,
    test_vectors,
    face_jacobians,
    wave_speed,
    viscosity,
    inverse_volume,
    connectivity,
    send_rows,
    cell_count,
):
    rows, cols = mesh_shape
    fields, vectors, cells = test_vectors.shape
    slots = send_rows.shape[1]
    groups = vectors // sublanes
    assert cells == lanes and groups * slots == lanes and 2 * vectors == lanes
    vmem = pl.BlockSpec(memory_space=pltpu.VMEM)
    speed = wave_speed.reshape(1, cells)
    visc = viscosity.reshape(1, cells)
    volume = inverse_volume.reshape(1, cells)
    state = jax.ShapeDtypeStruct(test_vectors.shape, jnp.float32)
    block = jax.ShapeDtypeStruct((fields, sublanes, lanes), jnp.float32)
    coefs = jax.ShapeDtypeStruct((4 * fields * fields, lanes), jnp.float32)
    tables = [
        jax.ShapeDtypeStruct((2, sublanes, lanes), jnp.float32),
        jax.ShapeDtypeStruct((4, sublanes, lanes), jnp.int32),
        jax.ShapeDtypeStruct((4, vectors, lanes), jnp.int32),
        coefs,
        coefs,
    ]
    params = pltpu.CompilerParams(vmem_limit_bytes=16 * 1024 * 1024)
    pairs = matchings(rows, cols)

    def exchange(sent):
        got = [None] * 4
        for which in arrival:
            got[which] = lax.ppermute(sent[which], ("gx", "gy"), pairs[which])
        return got

    ahead = pl.CostEstimate(flops=4 * 10**9, bytes_accessed=8 * 10**6, transcendentals=0)
    tile = jax.ShapeDtypeStruct((sublanes, lanes), jnp.int32)
    group = pl.pallas_call(
        functools.partial(groups_kernel, slots),
        out_shape=tile,
        out_specs=vmem,
        compiler_params=params,
        cost_estimate=ahead,
        name="groups",
    )()
    send_table, *sent = pl.pallas_call(
        prepare_kernel,
        out_shape=[jax.ShapeDtypeStruct((vectors, lanes), jnp.int32)] + [block] * 4,
        in_specs=[vmem] * 3,
        out_specs=[vmem] * 5,
        compiler_params=params,
        name="prepare",
    )(group, test_vectors, send_rows)
    centre, inside, outside, own_coef, ghost_coef = pl.pallas_call(
        functools.partial(tables_kernel, slots),
        out_shape=tables,
        in_specs=[vmem] * 6,
        out_specs=[vmem] * 5,
        compiler_params=params,
        name="tables",
    )(
        cell_count.reshape(1, 1),
        face_jacobians.transpose(1, 0, 2),
        connectivity,
        speed,
        visc,
        volume,
    )
    held = []
    for stage in range(4):
        last = stage == 3
        got = exchange(sent)
        partial = pl.pallas_call(
            functools.partial(own_kernel, stage),
            out_shape=[state] * (1 if last else 2),
            in_specs=[vmem] * (4 + len(held)),
            out_specs=[vmem] * (1 if last else 2),
            compiler_params=params,
            name="own",
        )(centre, inside, own_coef, test_vectors, *held)
        gram_shape = jax.ShapeDtypeStruct((vectors // 2, lanes), jnp.float32)
        result = pl.pallas_call(
            functools.partial(ghost_kernel, stage),
            out_shape=[state, gram_shape] if last else [state, state] + [block] * 4,
            in_specs=[vmem] * (5 + len(partial) + 4),
            out_specs=[vmem] * (2 if last else 6),
            compiler_params=params,
            name="ghost",
        )(outside, ghost_coef, centre, group, send_table, *partial, *[got[b] for b in arrival])
        held, sent = result[1::-1], result[2:]
    gram, advanced = held
    gram = summed(gram, rows, cols)
    scale = 1.0 / float(fields * cells * rows * cols)
    return pl.pallas_call(
        functools.partial(factor_kernel, scale),
        out_shape=[state, jax.ShapeDtypeStruct((vectors, vectors), jnp.float32)],
        in_specs=[vmem] * 2,
        out_specs=[vmem] * 2,
        compiler_params=params,
        name="factor",
    )(gram, advanced)


def solution(mesh):
    placed = (
        P(None, None, ("gx", "gy")),
        P(),
        P(("gx", "gy")),
        P(("gx", "gy")),
        P(("gx", "gy")),
        P(None, ("gx", "gy")),
        P(None, ("gx", "gy")),
        P(("gx", "gy")),
    )
    return jax.shard_map(
        functools.partial(shards, (mesh.shape["gx"], mesh.shape["gy"])),
        mesh=mesh,
        in_specs=placed,
        out_specs=(P(None, None, ("gx", "gy")), P()),
        check_vma=False,
    )
```

```python
import functools

import jax
import jax.numpy as jnp
from jax import lax
from jax.experimental import pallas as pl
from jax.experimental.pallas import tpu as pltpu
from jax.sharding import PartitionSpec as P

time_step = 0.4
slope_coef = (0.5 * time_step, 0.5 * time_step, time_step, time_step / 6.0)
arrival = (1, 2, 3, 0)
lanes = 128
sublanes = 8
HIGHEST = lax.Precision.HIGHEST


def partner(index, count, odd):
    other = index + 1 if index % 2 == odd else index - 1
    return other if 0 <= other < count else None


def matchings(rows, cols):
    row_even, row_odd, col_even, col_odd = [], [], [], []
    for i in range(rows):
        for j in range(cols):
            here = i * cols + j
            row_even.append((here, (i ^ 1) * cols + j))
            col_even.append((here, i * cols + (j ^ 1)))
            up = partner(i, rows, 1)
            row_odd.append((here, (rows - 1 - i if up is None else up) * cols + j))
            across = partner(j, cols, 1)
            col_odd.append((here, (i ^ 1) * cols + j if across is None else i * cols + across))
    return row_even, row_odd, col_even, col_odd


def lane_take(values, index):
    return jnp.take_along_axis(values, index, axis=1, mode="promise_in_bounds")


def lane_ids():
    return lax.broadcasted_iota(jnp.int32, (sublanes, lanes), 1)


def pack(states, group, send_table_ref, out_refs, groups):
    fields = len(states[0])
    packed = [[None] * fields for _ in range(4)]
    for m in range(groups):
        index = send_table_ref[pl.ds(m * sublanes, sublanes), :]
        for f in range(fields):
            taken = lane_take(states[m][f], index)
            for b in range(4):
                before = packed[b][f]
                packed[b][f] = (
                    taken
                    if before is None
                    else jnp.where(group == (m + b) % groups, taken, before)
                )
    for b in range(4):
        for f in range(fields):
            out_refs[b][f] = packed[b][f]


def groups_kernel(slots, group_ref):
    group_ref[...] = lane_ids() // slots


def prepare_kernel(group_ref, q_ref, send_ref, send_table_ref, *out_refs):
    fields, vectors, _ = q_ref.shape
    slots = send_ref.shape[1]
    groups = lanes // slots
    shape = (sublanes, lanes)
    group = group_ref[...]
    row_even = lax.axis_index("gx") % 2 == 0
    col_even = lax.axis_index("gy") % 2 == 0
    sends = jnp.concatenate(
        [send_ref[...], jnp.zeros((4, lanes - slots), jnp.int32)], axis=1
    )
    spread = [jnp.broadcast_to(sends[b : b + 1], shape) for b in range(4)]
    ordered = [
        jnp.where(row_even, spread[1], spread[0]),
        jnp.where(row_even, spread[0], spread[1]),
        jnp.where(col_even, spread[3], spread[2]),
        jnp.where(col_even, spread[2], spread[3]),
    ]
    base = ordered[0]
    for b in range(1, 4):
        base = jnp.where(group == b, pltpu.roll(ordered[b], b * slots, 1), base)
    for m in range(groups):
        send_table_ref[pl.ds(m * sublanes, sublanes), :] = (
            pltpu.roll(base, m * slots, 1) if m else base
        )
    states = [
        [q_ref[f, pl.ds(m * sublanes, sublanes), :] for f in range(fields)] for m in range(groups)
    ]
    pack(states, group, send_table_ref, out_refs, groups)


def tables_kernel(
    slots,
    count_ref,
    jac_ref,
    conn_ref,
    speed_ref,
    visc_ref,
    volume_ref,
    centre_ref,
    inside_ref,
    outside_ref,
    own_coef_ref,
    ghost_coef_ref,
):
    cells = conn_ref.shape[1]
    fields = jac_ref.shape[0]
    groups = lanes // slots
    shape = (sublanes, lanes)
    row_swap = jnp.where(lax.axis_index("gx") % 2 == 0, slots, 0)
    col_swap = jnp.where(lax.axis_index("gy") % 2 == 0, slots, 0)
    volume = jnp.broadcast_to(volume_ref[...], shape)
    advect = -0.5 * jnp.broadcast_to(speed_ref[...], shape) * volume
    diffuse = jnp.broadcast_to(visc_ref[...], shape) * volume
    centre_ref[0] = -4.0 * diffuse
    centre_ref[1] = jnp.where(lane_ids() < jnp.broadcast_to(count_ref[...], shape), 1.0, 0.0)
    sub = lax.broadcasted_iota(jnp.int32, shape, 0)
    for face in range(4):
        entry = jnp.broadcast_to(conn_ref[pl.ds(face, 1), :], shape)
        owned = entry < cells
        far = entry >= cells + 4 * slots
        inside_ref[face] = jnp.bitwise_and(entry, lanes - 1)
        ghost = entry - cells
        ghost = jnp.where(
            ghost < 2 * slots,
            jnp.bitwise_xor(ghost, row_swap),
            jnp.where(ghost < 4 * slots, jnp.bitwise_xor(ghost, col_swap), ghost),
        )
        for m in range(groups):
            outside_ref[face, pl.ds(m * sublanes, sublanes), :] = jnp.bitwise_and(
                ghost + m * slots, lanes - 1
            )
        for j in range(fields):
            rows = pl.ds((face * fields + j) * fields, fields)
            jacobian = jnp.broadcast_to(jac_ref[:, face, pl.ds(j, 1)], (fields, lanes))
            coef = jacobian * advect[:fields] + jnp.where(sub == j, diffuse, 0.0)[:fields]
            own_coef_ref[rows, :] = jnp.where(owned[:fields], coef, 0.0)
            ghost_coef_ref[rows, :] = jnp.where((owned | far)[:fields], 0.0, coef)


def neighbours(near, coef_ref, totals, face):
    fields = len(near)
    for j in range(fields):
        for i in range(fields):
            at = (face * fields + j) * fields + i
            term = coef_ref[pl.ds(at, 1), :] * near[j]
            totals[i] = term if totals[i] is None else totals[i] + term


def own_kernel(stage, centre_ref, inside_ref, coef_ref, q_ref, *refs):
    *state_refs, part_ref = refs
    newest_ref = state_refs[-1] if state_refs else q_ref
    fields, vectors, _ = q_ref.shape
    for start in range(0, vectors, sublanes):
        rows = pl.ds(start, sublanes)
        own = [newest_ref[f, rows, :] for f in range(fields)]
        totals = [centre_ref[0] * own[f] for f in range(fields)]
        for face in range(4):
            near = [lane_take(own[f], inside_ref[face]) for f in range(fields)]
            neighbours(near, coef_ref, totals, face)
        for f in range(fields):
            beside = q_ref[f, rows, :]
            if stage == 3:
                second, third = (ref[f, rows, :] for ref in state_refs[:2])
                beside = (second + 2.0 * third + own[f] - beside) * (1.0 / 3.0)
            part_ref[f, rows, :] = beside + slope_coef[stage] * totals[f]


def ghost_kernel(stage, outside_ref, coef_ref, centre_ref, group_ref, send_table_ref, *refs):
    refs = list(refs)
    last = stage == 3
    part_ref = refs.pop(0)
    recv_refs = dict(zip(arrival, (refs.pop(0) for _ in range(4))))
    fields, vectors, _ = part_ref.shape
    groups = vectors // sublanes
    group = group_ref[...]
    states = []
    for m in range(groups):
        rows = pl.ds(m * sublanes, sublanes)
        ghosts = []
        for f in range(fields):
            block = recv_refs[0][f]
            for b in range(1, 4):
                block = jnp.where(group == (m + b) % groups, recv_refs[b][f], block)
            ghosts.append(block)
        totals = [None] * fields
        for face in range(4):
            near = [lane_take(ghosts[f], outside_ref[face, rows, :]) for f in range(fields)]
            neighbours(near, coef_ref, totals, face)
        following = []
        for f in range(fields):
            after = part_ref[f, rows, :] + slope_coef[stage] * totals[f]
            if last:
                after = after * centre_ref[1]
            refs[0][f, rows, :] = after
            following.append(after)
        states.append(following)
    if not last:
        pack(states, group, send_table_ref, refs[1:], groups)
        return
    half = vectors // 2
    wide = jnp.concatenate([refs[0][f] for f in range(fields)], axis=1)
    gram = lax.dot_general(
        wide,
        wide,
        (((1,), (1,)), ((), ())),
        precision=HIGHEST,
        preferred_element_type=jnp.float32,
    )
    gram = jnp.concatenate([gram, jnp.zeros_like(gram)], axis=1)
    refs[1][...] = gram[:half] + pltpu.roll(gram[half:], vectors, 1)


def factor_kernel(scale, gram_ref, advanced_ref, basis_hbm, factor_hbm, basis_ref, factor_ref, sem_ref):
    fields, vectors, cells = advanced_ref.shape
    folded = gram_ref[...] * scale
    work = jnp.concatenate([folded, pltpu.roll(folded, vectors, 1)], axis=0)
    row = lax.broadcasted_iota(jnp.int32, (vectors, lanes), 0)
    lane = lax.broadcasted_iota(jnp.int32, (vectors, lanes), 1)
    shape = (sublanes, lanes)
    sub = lax.broadcasted_iota(jnp.int32, shape, 0)
    diagonal = jnp.where(lane == row, work, 0.0)
    by_row = lax.rsqrt(jnp.sum(diagonal, axis=1, keepdims=True))
    by_lane = jnp.sum(diagonal, axis=0, keepdims=True)
    lane_root = lax.rsqrt(by_lane)
    work = jnp.where(
        lane < vectors,
        work * by_row * lane_root,
        jnp.where(lane == row + vectors, 1.0, 0.0),
    )
    restore = jnp.where(
        lane[:1] < vectors, by_lane * lane_root, pltpu.roll(lane_root, vectors, 1)
    )
    blocks = [work[at : at + sublanes] for at in range(0, vectors, sublanes)]

    def spread(tile, k):
        return jnp.broadcast_to(tile[k : k + 1], shape)

    for b in range(len(blocks)):
        start = b * sublanes
        later = range(b, len(blocks))
        columns = [
            [lane_take(blocks[c], jnp.full(shape, start + k, jnp.int32)) for c in later]
            for k in range(sublanes)
        ]
        pivots = None
        for k in range(0, sublanes, 2):
            left, right = columns[k], columns[k + 1]
            p, q, r = spread(left[0], k), spread(right[0], k), spread(right[0], k + 1)
            first = 1.0 / p
            second = p * (1.0 / (p * r - q * q))
            ratio = q * first
            right = [right[c] - ratio * left[c] for c in range(len(later))]
            top, bottom = spread(blocks[b], k), spread(blocks[b], k + 1)
            bottom = bottom - ratio * top
            upper, lower = top * first, bottom * second
            for n in range(k + 2, sublanes):
                high, low = spread(columns[n][0], k), spread(columns[n][0], k + 1)
                high, low = high * first, (low - ratio * high) * second
                for c in range(len(later)):
                    columns[n][c] = columns[n][c] - (left[c] * high + right[c] * low)
            for c in range(len(later)):
                change = left[c] * upper + right[c] * lower
                if c == 0:
                    change = jnp.where(sub > k + 1, change, jnp.where(sub == k + 1, ratio * top, 0.0))
                blocks[b + c] = blocks[b + c] - change
            pivots = p if pivots is None else jnp.where(sub >= k, p, pivots)
            pivots = jnp.where(sub > k, r - ratio * q, pivots)
        blocks[b] = blocks[b] * lax.rsqrt(pivots)
    done = jnp.concatenate(blocks, axis=0) * restore
    factor_ref[...] = jnp.where(lane >= row, done, 0.0)[:, :vectors]
    copies = [pltpu.make_async_copy(factor_ref, factor_hbm, sem_ref.at[fields])]
    copies[0].start()
    inverse_lower = pltpu.roll(done, vectors, 1)[:, :vectors]
    for f in range(fields):
        basis_ref[f] = jnp.dot(
            inverse_lower,
            advanced_ref[f],
            precision=HIGHEST,
            preferred_element_type=jnp.float32,
        )
        copies.append(pltpu.make_async_copy(basis_ref.at[f], basis_hbm.at[f], sem_ref.at[f]))
        copies[-1].start()
    for copy in copies:
        copy.wait()


def summed(value, rows, cols):
    steps = [(1, 0)]
    step = 2
    while step < rows:
        steps.append((step + 1, 0))
        step *= 2
    step = 1
    while step < cols:
        steps.append((1, step))
        step *= 2
    for across, along in steps:
        pairs = [
            (i * cols + j, (i ^ across) * cols + (j ^ along))
            for i in range(rows)
            for j in range(cols)
        ]
        value = value + lax.ppermute(value, ("gx", "gy"), pairs)
    return value


def shards(
    mesh_shape,
    test_vectors,
    face_jacobians,
    wave_speed,
    viscosity,
    inverse_volume,
    connectivity,
    send_rows,
    cell_count,
):
    rows, cols = mesh_shape
    fields, vectors, cells = test_vectors.shape
    slots = send_rows.shape[1]
    groups = vectors // sublanes
    assert cells == lanes and groups * slots == lanes and 2 * vectors == lanes
    vmem = pl.BlockSpec(memory_space=pltpu.VMEM)
    speed = wave_speed.reshape(1, cells)
    visc = viscosity.reshape(1, cells)
    volume = inverse_volume.reshape(1, cells)
    state = jax.ShapeDtypeStruct(test_vectors.shape, jnp.float32)
    block = jax.ShapeDtypeStruct((fields, sublanes, lanes), jnp.float32)
    coefs = jax.ShapeDtypeStruct((4 * fields * fields, lanes), jnp.float32)
    tables = [
        jax.ShapeDtypeStruct((2, sublanes, lanes), jnp.float32),
        jax.ShapeDtypeStruct((4, sublanes, lanes), jnp.int32),
        jax.ShapeDtypeStruct((4, vectors, lanes), jnp.int32),
        coefs,
        coefs,
    ]
    params = pltpu.CompilerParams(vmem_limit_bytes=16 * 1024 * 1024)
    pairs = matchings(rows, cols)

    def exchange(sent):
        got = [None] * 4
        for which in arrival:
            got[which] = lax.ppermute(sent[which], ("gx", "gy"), pairs[which])
        return got

    ahead = pl.CostEstimate(flops=4 * 10**9, bytes_accessed=8 * 10**6, transcendentals=0)
    tile = jax.ShapeDtypeStruct((sublanes, lanes), jnp.int32)
    group = pl.pallas_call(
        functools.partial(groups_kernel, slots),
        out_shape=tile,
        out_specs=vmem,
        compiler_params=params,
        cost_estimate=ahead,
        name="groups",
    )()
    send_table, *sent = pl.pallas_call(
        prepare_kernel,
        out_shape=[jax.ShapeDtypeStruct((vectors, lanes), jnp.int32)] + [block] * 4,
        in_specs=[vmem] * 3,
        out_specs=[vmem] * 5,
        compiler_params=params,
        name="prepare",
    )(group, test_vectors, send_rows)
    centre, inside, outside, own_coef, ghost_coef = pl.pallas_call(
        functools.partial(tables_kernel, slots),
        out_shape=tables,
        in_specs=[vmem] * 6,
        out_specs=[vmem] * 5,
        compiler_params=params,
        name="tables",
    )(
        cell_count.reshape(1, 1),
        face_jacobians.transpose(1, 0, 2),
        connectivity,
        speed,
        visc,
        volume,
    )
    held = []
    for stage in range(4):
        last = stage == 3
        got = exchange(sent)
        partial = pl.pallas_call(
            functools.partial(own_kernel, stage),
            out_shape=state,
            in_specs=[vmem] * (4 + len(held)),
            out_specs=vmem,
            compiler_params=params,
            name="own",
        )(centre, inside, own_coef, test_vectors, *held)
        gram_shape = jax.ShapeDtypeStruct((vectors // 2, lanes), jnp.float32)
        newest, *sent = pl.pallas_call(
            functools.partial(ghost_kernel, stage),
            out_shape=[state, gram_shape] if last else [state] + [block] * 4,
            in_specs=[vmem] * 10,
            out_specs=[vmem] * (2 if last else 5),
            compiler_params=params,
            name="ghost",
        )(outside, ghost_coef, centre, group, send_table, partial, *[got[b] for b in arrival])
        held.append(newest)
    advanced, gram = held[-1], sent[0]
    gram = summed(gram, rows, cols)
    scale = 1.0 / float(fields * cells * rows * cols)
    lower = jax.ShapeDtypeStruct((vectors, vectors), jnp.float32)
    hbm = pl.BlockSpec(memory_space=pltpu.HBM)
    return pl.pallas_call(
        functools.partial(factor_kernel, scale),
        out_shape=[state, lower],
        in_specs=[vmem] * 2,
        out_specs=[hbm] * 2,
        scratch_shapes=[
            pltpu.VMEM(state.shape, jnp.float32),
            pltpu.VMEM(lower.shape, jnp.float32),
            pltpu.SemaphoreType.DMA((fields + 1,)),
        ],
        compiler_params=params,
        name="factor",
    )(gram, advanced)


def solution(mesh):
    placed = (
        P(None, None, ("gx", "gy")),
        P(),
        P(("gx", "gy")),
        P(("gx", "gy")),
        P(("gx", "gy")),
        P(None, ("gx", "gy")),
        P(None, ("gx", "gy")),
        P(("gx", "gy")),
    )
    return jax.shard_map(
        functools.partial(shards, (mesh.shape["gx"], mesh.shape["gy"])),
        mesh=mesh,
        in_specs=placed,
        out_specs=(P(None, None, ("gx", "gy")), P()),
        check_vma=False,
    )
```

```python
import functools

import jax
import jax.numpy as jnp
from jax import lax
from jax.experimental import pallas as pl
from jax.experimental.pallas import tpu as pltpu
from jax.sharding import PartitionSpec as P

time_step = 0.4
slope_coef = (0.5 * time_step, 0.5 * time_step, time_step, time_step / 6.0)
arrival = (1, 2, 3, 0)
lanes = 128
sublanes = 8
HIGHEST = lax.Precision.HIGHEST


def partner(index, count, odd):
    other = index + 1 if index % 2 == odd else index - 1
    return other if 0 <= other < count else None


def matchings(rows, cols):
    row_even, row_odd, col_even, col_odd = [], [], [], []
    for i in range(rows):
        for j in range(cols):
            here = i * cols + j
            row_even.append((here, (i ^ 1) * cols + j))
            col_even.append((here, i * cols + (j ^ 1)))
            up = partner(i, rows, 1)
            row_odd.append((here, (rows - 1 - i if up is None else up) * cols + j))
            across = partner(j, cols, 1)
            col_odd.append((here, (i ^ 1) * cols + j if across is None else i * cols + across))
    return row_even, row_odd, col_even, col_odd


def lane_take(values, index):
    return jnp.take_along_axis(values, index, axis=1, mode="promise_in_bounds")


def lane_ids():
    return lax.broadcasted_iota(jnp.int32, (sublanes, lanes), 1)


def pack(states, group, send_table_ref, out_refs, groups):
    fields = len(states[0])
    packed = [[None] * fields for _ in range(4)]
    for m in range(groups):
        index = send_table_ref[pl.ds(m * sublanes, sublanes), :]
        for f in range(fields):
            taken = lane_take(states[m][f], index)
            for b in range(4):
                before = packed[b][f]
                packed[b][f] = (
                    taken
                    if before is None
                    else jnp.where(group == (m + b) % groups, taken, before)
                )
    for b in range(4):
        for f in range(fields):
            out_refs[b][f] = packed[b][f]


def groups_kernel(slots, group_ref):
    group_ref[...] = lane_ids() // slots


def prepare_kernel(group_ref, q_ref, send_ref, send_table_ref, *out_refs):
    fields, vectors, _ = q_ref.shape
    slots = send_ref.shape[1]
    groups = lanes // slots
    shape = (sublanes, lanes)
    group = group_ref[...]
    row_even = lax.axis_index("gx") % 2 == 0
    col_even = lax.axis_index("gy") % 2 == 0
    sends = jnp.concatenate(
        [send_ref[...], jnp.zeros((4, lanes - slots), jnp.int32)], axis=1
    )
    spread = [jnp.broadcast_to(sends[b : b + 1], shape) for b in range(4)]
    ordered = [
        jnp.where(row_even, spread[1], spread[0]),
        jnp.where(row_even, spread[0], spread[1]),
        jnp.where(col_even, spread[3], spread[2]),
        jnp.where(col_even, spread[2], spread[3]),
    ]
    base = ordered[0]
    for b in range(1, 4):
        base = jnp.where(group == b, pltpu.roll(ordered[b], b * slots, 1), base)
    for m in range(groups):
        send_table_ref[pl.ds(m * sublanes, sublanes), :] = (
            pltpu.roll(base, m * slots, 1) if m else base
        )
    states = [
        [q_ref[f, pl.ds(m * sublanes, sublanes), :] for f in range(fields)] for m in range(groups)
    ]
    pack(states, group, send_table_ref, out_refs, groups)


def tables_kernel(
    slots,
    count_ref,
    jac_ref,
    conn_ref,
    speed_ref,
    visc_ref,
    volume_ref,
    centre_ref,
    inside_ref,
    outside_ref,
    own_coef_ref,
    ghost_coef_ref,
):
    cells = conn_ref.shape[1]
    fields = jac_ref.shape[0]
    groups = lanes // slots
    shape = (sublanes, lanes)
    row_swap = jnp.where(lax.axis_index("gx") % 2 == 0, slots, 0)
    col_swap = jnp.where(lax.axis_index("gy") % 2 == 0, slots, 0)
    volume = jnp.broadcast_to(volume_ref[...], shape)
    advect = -0.5 * jnp.broadcast_to(speed_ref[...], shape) * volume
    diffuse = jnp.broadcast_to(visc_ref[...], shape) * volume
    centre_ref[0] = -4.0 * diffuse
    centre_ref[1] = jnp.where(lane_ids() < jnp.broadcast_to(count_ref[...], shape), 1.0, 0.0)
    sub = lax.broadcasted_iota(jnp.int32, shape, 0)
    for face in range(4):
        entry = jnp.broadcast_to(conn_ref[pl.ds(face, 1), :], shape)
        owned = entry < cells
        far = entry >= cells + 4 * slots
        inside_ref[face] = jnp.bitwise_and(entry, lanes - 1)
        ghost = entry - cells
        ghost = jnp.where(
            ghost < 2 * slots,
            jnp.bitwise_xor(ghost, row_swap),
            jnp.where(ghost < 4 * slots, jnp.bitwise_xor(ghost, col_swap), ghost),
        )
        for m in range(groups):
            outside_ref[face, pl.ds(m * sublanes, sublanes), :] = jnp.bitwise_and(
                ghost + m * slots, lanes - 1
            )
        for j in range(fields):
            rows = pl.ds((face * fields + j) * fields, fields)
            jacobian = jnp.broadcast_to(jac_ref[:, face, pl.ds(j, 1)], (fields, lanes))
            coef = jacobian * advect[:fields] + jnp.where(sub == j, diffuse, 0.0)[:fields]
            own_coef_ref[rows, :] = jnp.where(owned[:fields], coef, 0.0)
            ghost_coef_ref[rows, :] = jnp.where((owned | far)[:fields], 0.0, coef)


def first_kernel(slots, *refs):
    small_refs, q_ref, table_refs, part_ref = refs[:6], refs[6], refs[7:12], refs[12]
    tables_kernel(slots, *small_refs, *table_refs)
    centre_ref, inside_ref, _, own_coef_ref, _ = table_refs
    own_kernel(0, centre_ref, inside_ref, own_coef_ref, q_ref, part_ref)


def neighbours(near, coef_ref, totals, face):
    fields = len(near)
    for j in range(fields):
        for i in range(fields):
            at = (face * fields + j) * fields + i
            term = coef_ref[pl.ds(at, 1), :] * near[j]
            totals[i] = term if totals[i] is None else totals[i] + term


def own_kernel(stage, centre_ref, inside_ref, coef_ref, q_ref, *refs):
    *state_refs, part_ref = refs
    newest_ref = state_refs[-1] if state_refs else q_ref
    fields, vectors, _ = q_ref.shape
    for start in range(0, vectors, sublanes):
        rows = pl.ds(start, sublanes)
        own = [newest_ref[f, rows, :] for f in range(fields)]
        totals = [centre_ref[0] * own[f] for f in range(fields)]
        for face in range(4):
            near = [lane_take(own[f], inside_ref[face]) for f in range(fields)]
            neighbours(near, coef_ref, totals, face)
        for f in range(fields):
            beside = q_ref[f, rows, :]
            if stage == 3:
                second, third = (ref[f, rows, :] for ref in state_refs[:2])
                beside = (second + 2.0 * third + own[f] - beside) * (1.0 / 3.0)
            part_ref[f, rows, :] = beside + slope_coef[stage] * totals[f]


def ghost_kernel(stage, outside_ref, coef_ref, centre_ref, group_ref, send_table_ref, *refs):
    refs = list(refs)
    last = stage == 3
    part_ref = refs.pop(0)
    recv_refs = dict(zip(arrival, (refs.pop(0) for _ in range(4))))
    fields, vectors, _ = part_ref.shape
    groups = vectors // sublanes
    group = group_ref[...]
    states = []
    for m in range(groups):
        rows = pl.ds(m * sublanes, sublanes)
        ghosts = []
        for f in range(fields):
            block = recv_refs[0][f]
            for b in range(1, 4):
                block = jnp.where(group == (m + b) % groups, recv_refs[b][f], block)
            ghosts.append(block)
        totals = [None] * fields
        for face in range(4):
            near = [lane_take(ghosts[f], outside_ref[face, rows, :]) for f in range(fields)]
            neighbours(near, coef_ref, totals, face)
        following = []
        for f in range(fields):
            after = part_ref[f, rows, :] + slope_coef[stage] * totals[f]
            if last:
                after = after * centre_ref[1]
            refs[0][f, rows, :] = after
            following.append(after)
        states.append(following)
    if not last:
        pack(states, group, send_table_ref, refs[1:], groups)
        return
    half = vectors // 2
    wide = jnp.concatenate([refs[0][f] for f in range(fields)], axis=1)
    gram = lax.dot_general(
        wide,
        wide,
        (((1,), (1,)), ((), ())),
        precision=HIGHEST,
        preferred_element_type=jnp.float32,
    )
    gram = jnp.concatenate([gram, jnp.zeros_like(gram)], axis=1)
    refs[1][...] = gram[:half] + pltpu.roll(gram[half:], vectors, 1)


def factor_kernel(scale, gram_ref, advanced_ref, basis_hbm, factor_hbm, basis_ref, factor_ref, sem_ref):
    fields, vectors, cells = advanced_ref.shape
    folded = gram_ref[...] * scale
    work = jnp.concatenate([folded, pltpu.roll(folded, vectors, 1)], axis=0)
    row = lax.broadcasted_iota(jnp.int32, (vectors, lanes), 0)
    lane = lax.broadcasted_iota(jnp.int32, (vectors, lanes), 1)
    shape = (sublanes, lanes)
    sub = lax.broadcasted_iota(jnp.int32, shape, 0)
    diagonal = jnp.where(lane == row, work, 0.0)
    by_row = jnp.broadcast_to(
        lax.rsqrt(jnp.sum(diagonal, axis=1, keepdims=True)), (vectors, lanes)
    )
    by_lane = jnp.sum(diagonal, axis=0, keepdims=True)
    lane_root = lax.rsqrt(by_lane)
    work = jnp.where(lane < vectors, work * by_row * lane_root, 0.0)
    blocks = []
    for at in range(0, vectors, sublanes):
        here = [work[at : at + sublanes]]
        for f in range(fields):
            here.append(advanced_ref[f, pl.ds(at, sublanes), :] * by_row[at : at + sublanes])
        blocks.append(here)

    def spread(tile, k):
        return jnp.broadcast_to(tile[k : k + 1], shape)

    copies = []
    done = []
    for b in range(len(blocks)):
        start = b * sublanes
        later = range(b, len(blocks))
        columns = [
            [lane_take(blocks[c][0], jnp.full(shape, start + k, jnp.int32)) for c in later]
            for k in range(sublanes)
        ]
        pivots = None
        for k in range(0, sublanes, 2):
            left, right = columns[k], columns[k + 1]
            p, q, r = spread(left[0], k), spread(right[0], k), spread(right[0], k + 1)
            first = 1.0 / p
            second = p * (1.0 / (p * r - q * q))
            ratio = q * first
            right = [right[c] - ratio * left[c] for c in range(len(later))]
            for n in range(k + 2, sublanes):
                high, low = spread(columns[n][0], k), spread(columns[n][0], k + 1)
                high, low = high * first, (low - ratio * high) * second
                for c in range(len(later)):
                    columns[n][c] = columns[n][c] - (left[c] * high + right[c] * low)
            for t in range(1 + fields):
                top = spread(blocks[b][t], k)
                upper = top * first
                lower = (spread(blocks[b][t], k + 1) - ratio * top) * second
                for c in range(len(later)):
                    change = left[c] * upper + right[c] * lower
                    if c == 0:
                        change = jnp.where(
                            sub > k + 1, change, jnp.where(sub == k + 1, ratio * top, 0.0)
                        )
                    blocks[b + c][t] = blocks[b + c][t] - change
            pivots = p if pivots is None else jnp.where(sub >= k, p, pivots)
            pivots = jnp.where(sub > k, r - ratio * q, pivots)
        root = lax.rsqrt(pivots)
        rows = pl.ds(start, sublanes)
        done.append(blocks[b][0] * root)
        for f in range(fields):
            basis_ref[f, rows, :] = blocks[b][1 + f] * root
        copies.append(
            pltpu.make_async_copy(
                basis_ref.at[:, rows, :], basis_hbm.at[:, rows, :], sem_ref.at[b]
            )
        )
        copies[-1].start()
    upper = jnp.concatenate(done, axis=0) * (by_lane * lane_root)
    factor_ref[...] = jnp.where(lane >= row, upper, 0.0)[:, :vectors]
    copies.append(pltpu.make_async_copy(factor_ref, factor_hbm, sem_ref.at[len(blocks)]))
    copies[-1].start()
    for copy in copies:
        copy.wait()


def summed(value, rows, cols):
    steps = [(1, 0)]
    step = 2
    while step < rows:
        steps.append((step + 1, 0))
        step *= 2
    step = 1
    while step < cols:
        steps.append((1, step))
        step *= 2
    for across, along in steps:
        pairs = [
            (i * cols + j, (i ^ across) * cols + (j ^ along))
            for i in range(rows)
            for j in range(cols)
        ]
        value = value + lax.ppermute(value, ("gx", "gy"), pairs)
    return value


def shards(
    mesh_shape,
    test_vectors,
    face_jacobians,
    wave_speed,
    viscosity,
    inverse_volume,
    connectivity,
    send_rows,
    cell_count,
):
    rows, cols = mesh_shape
    fields, vectors, cells = test_vectors.shape
    slots = send_rows.shape[1]
    groups = vectors // sublanes
    assert cells == lanes and groups * slots == lanes and 2 * vectors == lanes
    vmem = pl.BlockSpec(memory_space=pltpu.VMEM)
    speed = wave_speed.reshape(1, cells)
    visc = viscosity.reshape(1, cells)
    volume = inverse_volume.reshape(1, cells)
    state = jax.ShapeDtypeStruct(test_vectors.shape, jnp.float32)
    block = jax.ShapeDtypeStruct((fields, sublanes, lanes), jnp.float32)
    coefs = jax.ShapeDtypeStruct((4 * fields * fields, lanes), jnp.float32)
    tables = [
        jax.ShapeDtypeStruct((2, sublanes, lanes), jnp.float32),
        jax.ShapeDtypeStruct((4, sublanes, lanes), jnp.int32),
        jax.ShapeDtypeStruct((4, vectors, lanes), jnp.int32),
        coefs,
        coefs,
    ]
    params = pltpu.CompilerParams(vmem_limit_bytes=16 * 1024 * 1024)
    pairs = matchings(rows, cols)

    def exchange(sent):
        got = [None] * 4
        for which in arrival:
            got[which] = lax.ppermute(sent[which], ("gx", "gy"), pairs[which])
        return got

    ahead = pl.CostEstimate(flops=4 * 10**9, bytes_accessed=8 * 10**6, transcendentals=0)
    tile = jax.ShapeDtypeStruct((sublanes, lanes), jnp.int32)
    group = pl.pallas_call(
        functools.partial(groups_kernel, slots),
        out_shape=tile,
        out_specs=vmem,
        compiler_params=params,
        cost_estimate=ahead,
        name="groups",
    )()
    send_table, *sent = pl.pallas_call(
        prepare_kernel,
        out_shape=[jax.ShapeDtypeStruct((vectors, lanes), jnp.int32)] + [block] * 4,
        in_specs=[vmem] * 3,
        out_specs=[vmem] * 5,
        compiler_params=params,
        name="prepare",
    )(group, test_vectors, send_rows)
    centre, inside, outside, own_coef, ghost_coef, partial = pl.pallas_call(
        functools.partial(first_kernel, slots),
        out_shape=tables + [state],
        in_specs=[vmem] * 7,
        out_specs=[vmem] * 6,
        compiler_params=params,
        name="tables",
    )(
        cell_count.reshape(1, 1),
        face_jacobians.transpose(1, 0, 2),
        connectivity,
        speed,
        visc,
        volume,
        test_vectors,
    )
    held = []
    for stage in range(4):
        last = stage == 3
        got = exchange(sent)
        if stage > 0:
            partial = pl.pallas_call(
                functools.partial(own_kernel, stage),
                out_shape=state,
                in_specs=[vmem] * (4 + len(held)),
                out_specs=vmem,
                compiler_params=params,
                name="own",
            )(centre, inside, own_coef, test_vectors, *held)
        gram_shape = jax.ShapeDtypeStruct((vectors // 2, lanes), jnp.float32)
        newest, *sent = pl.pallas_call(
            functools.partial(ghost_kernel, stage),
            out_shape=[state, gram_shape] if last else [state] + [block] * 4,
            in_specs=[vmem] * 10,
            out_specs=[vmem] * (2 if last else 5),
            compiler_params=params,
            name="ghost",
        )(outside, ghost_coef, centre, group, send_table, partial, *[got[b] for b in arrival])
        held.append(newest)
    advanced, gram = held[-1], sent[0]
    gram = summed(gram, rows, cols)
    scale = 1.0 / float(fields * cells * rows * cols)
    lower = jax.ShapeDtypeStruct((vectors, vectors), jnp.float32)
    hbm = pl.BlockSpec(memory_space=pltpu.HBM)
    return pl.pallas_call(
        functools.partial(factor_kernel, scale),
        out_shape=[state, lower],
        in_specs=[vmem] * 2,
        out_specs=[hbm] * 2,
        scratch_shapes=[
            pltpu.VMEM(state.shape, jnp.float32),
            pltpu.VMEM(lower.shape, jnp.float32),
            pltpu.SemaphoreType.DMA((vectors // sublanes + 1,)),
        ],
        compiler_params=params,
        name="factor",
    )(gram, advanced)


def solution(mesh):
    placed = (
        P(None, None, ("gx", "gy")),
        P(),
        P(("gx", "gy")),
        P(("gx", "gy")),
        P(("gx", "gy")),
        P(None, ("gx", "gy")),
        P(None, ("gx", "gy")),
        P(("gx", "gy")),
    )
    return jax.shard_map(
        functools.partial(shards, (mesh.shape["gx"], mesh.shape["gy"])),
        mesh=mesh,
        in_specs=placed,
        out_specs=(P(None, None, ("gx", "gy")), P()),
        check_vma=False,
    )
```
